256 devices in a mesh: dp: 64 (over z, y, core), proto: 4 (over x).
Axes of the slice: x: 4, y: 4, z: 8, core: 2. Of those that a mesh axis runs over, the one named last changes fastest.
Arguments:
- student_feat: bfloat16 [16384, 256], P('dp'), may hold values from -6 to 6
- teacher_feat: bfloat16 [16384, 256], P('dp'), may hold values from -6 to 6
- prototypes: bfloat16 [65536, 256], P(('dp', 'proto')), may hold values from -6 to 6
Outputs:
- grad_student: float32 [16384, 256], P('dp')
- grad_proto: float32 [65536, 256], P(('dp', 'proto'))
The draws below stay inside these ranges and needn't reach their ends.
All inputs are finite; a program needn't handle non-finite values.
Results may differ from the reference program's by a relative error of at most 0.0041.
Values may be sent and summed in bfloat16 or wider, within the bound.
A program may use at most 128 MiB of HBM per device.

```python
import jax
import jax.numpy as jnp
from jax import lax

FEATURES = 256
PROTOS = 65536
SWEEPS = 3
CROP_DEV = 256
CROPS = 16384
N_DP = 64


def cluster_axes(key):
    table_key = jax.random.fold_in(key, 101)
    return jnp.clip(jax.random.normal(table_key, (64, FEATURES), jnp.float32), -3.0, 3.0)


def crop_members(key):
    member_key = jax.random.fold_in(key, 202)
    first_key, second_key, third_key = jax.random.split(member_key, 3)
    first = jax.random.randint(first_key, (CROPS,), 0, 64)
    second = jax.random.randint(second_key, (CROPS,), 0, 64)
    third = jax.random.randint(third_key, (CROPS,), 0, 64)
    return jnp.minimum(jnp.minimum(first, second), third)


def crop_centres(key):
    axes_table = cluster_axes(key)
    return axes_table[crop_members(key)]


def compose(centre, noise):
    return centre + noise


def draw_student_feat(key, part):
    centre = crop_centres(key)
    key = jax.random.fold_in(key, 7)
    noise = 0.7 * jnp.clip(jax.random.normal(key, (CROPS, FEATURES), jnp.float32), -3.0, 3.0)
    return compose(centre, noise).astype(jnp.bfloat16)


def draw_teacher_feat(key, part):
    centre = crop_centres(key)
    key = jax.random.fold_in(key, 11)
    noise = 0.7 * jnp.clip(jax.random.normal(key, (CROPS, FEATURES), jnp.float32), -3.0, 3.0)
    return compose(centre, noise).astype(jnp.bfloat16)


def draw_prototypes(key, part):
    axes_table = cluster_axes(key)
    key = jax.random.fold_in(key, 13)
    owner_key, aligned_key, noise_key = jax.random.split(key, 3)
    owner = jax.random.randint(owner_key, (PROTOS,), 0, 64)
    aligned = jax.random.randint(aligned_key, (PROTOS, 1), 0, 4) < 3
    centre = jnp.where(aligned, axes_table[owner], 0.0)
    noise = 0.7 * jnp.clip(jax.random.normal(noise_key, (PROTOS, FEATURES), jnp.float32), -3.0, 3.0)
    return compose(centre, noise).astype(jnp.bfloat16)


def setup_inputs(seed: int = 0) -> dict:
    key_of = jax.random.split(jax.random.key(seed), 4)
    student_feat = draw_student_feat(jax.random.fold_in(key_of[3], 71), 0)
    teacher_feat = draw_teacher_feat(jax.random.fold_in(key_of[3], 71), 0)
    prototypes = draw_prototypes(jax.random.fold_in(key_of[3], 71), 0)
    return dict(student_feat=student_feat, teacher_feat=teacher_feat, prototypes=prototypes)


teacher_temp = 0.07
student_temp = 0.1
loss_scale = 1024.0
epsilon = 1e-06

def unit_rows(matrix):
    values = matrix.astype(jnp.float32)
    inverse = lax.rsqrt(lax.optimization_barrier(jnp.sum(values * values, axis=-1, keepdims=True)) + epsilon)
    return (values * inverse, inverse)

def reference(student_feat, teacher_feat, prototypes):
    student_unit, student_inverse = unit_rows(student_feat)
    student_bf = student_unit.astype(jnp.bfloat16)
    teacher_unit, teacher_inverse = unit_rows(teacher_feat)
    teacher_bf = teacher_unit.astype(jnp.bfloat16)
    proto_unit, proto_inverse = unit_rows(prototypes)
    proto_bf = proto_unit.astype(jnp.bfloat16)
    contract = (((1,), (1,)), ((), ()))
    teacher_exp = jnp.exp(lax.dot_general(teacher_bf, proto_bf, contract, preferred_element_type=jnp.float32) / teacher_temp)
    row_scale = jnp.ones((CROPS,), jnp.float32)
    col_scale = jnp.ones((PROTOS,), jnp.float32)
    for sweep_index in range(SWEEPS):
        col_total = jnp.dot(row_scale, teacher_exp, precision=lax.Precision.HIGHEST)
        col_scale = 1.0 / (PROTOS * col_total)
        row_total = jnp.dot(teacher_exp, col_scale, precision=lax.Precision.HIGHEST)
        row_scale = 1.0 / (CROPS * row_total)
    exp_blocks = teacher_exp.reshape(N_DP, CROP_DEV, PROTOS)
    scale_blocks = row_scale.reshape(N_DP, CROP_DEV)
    bf_blocks = student_bf.reshape(N_DP, CROP_DEV, FEATURES)
    unit_blocks = student_unit.reshape(N_DP, CROP_DEV, FEATURES)
    inverse_blocks = student_inverse.reshape(N_DP, CROP_DEV, 1)

    def row_step(running, inputs):
        exp_rows, scale_rows, bf_rows, unit_rows32, inverse_rows = inputs
        targets = CROPS * exp_rows * scale_rows[:, None] * col_scale[None, :]
        student_exp = jnp.exp(lax.dot_general(bf_rows, proto_bf, contract, preferred_element_type=jnp.float32) / student_temp)
        partition = lax.optimization_barrier(jnp.sum(student_exp, axis=1, keepdims=True))
        logit_grad = (loss_scale * (student_exp / partition - targets) / student_temp).astype(jnp.bfloat16)
        unit_grad = jnp.dot(logit_grad, proto_bf, preferred_element_type=jnp.float32)
        grad_rows = inverse_rows * (unit_grad - unit_rows32 * lax.optimization_barrier(jnp.sum(unit_rows32 * unit_grad, axis=1, keepdims=True)))
        running = running + lax.dot_general(logit_grad, bf_rows, (((0,), (0,)), ((), ())), preferred_element_type=jnp.float32)
        return (running, grad_rows)
    start_acc = jnp.zeros((PROTOS, FEATURES), jnp.float32)
    proto_unit_grad, grad_blocks = lax.scan(row_step, start_acc, (exp_blocks, scale_blocks, bf_blocks, unit_blocks, inverse_blocks))
    grad_student = grad_blocks.reshape(CROPS, FEATURES)
    grad_proto = proto_inverse * (proto_unit_grad - proto_unit * lax.optimization_barrier(jnp.sum(proto_unit * proto_unit_grad, axis=1, keepdims=True)))
    return (grad_student, grad_proto)
```

```python
import functools
import math

import jax
import jax.numpy as jnp
from jax import lax
from jax.experimental import pallas as pl
from jax.experimental.pallas import tpu as pltpu
from jax.sharding import PartitionSpec as P

NZ, NY, NX, NC = 8, 4, 4, 2
B = 256
ROWS = NY * NC * B
COLS = NZ * B
CROPS = 16384
PROTOS = 65536
SWEEPS = 3
teacher_temp = 0.07
student_temp = 0.1
loss_scale = 1024.0
epsilon = 1e-06
LOG2E = math.log2(math.e)
MESH = pl.DeviceIdType.MESH
NT = (((1,), (1,)), ((), ()))
f32 = jnp.float32
bf16 = jnp.bfloat16
SUB = 4
PIECE = B // SUB
TILE = 512


def unit_rows(matrix):
    values = matrix.astype(f32)
    inverse = lax.rsqrt(jnp.sum(values * values, axis=-1, keepdims=True) + epsilon)
    return values * inverse, inverse


def kernel(
    student_ref, teacher_ref, proto_ref, gs_ref, gp_ref,
    protos, teach, stud, stud_t, t_exp, s_exp, grad, part, row_a, row_b, mat,
    col_send, col_recv, row_sib, row_send, sib_recv, row_recv,
    chunk, ring_send, ring_recv, u_ref, u_send, u_sib, v_send, v_recv, q_send, q_full,
    ag_ss, ag_rs, cr_ss, cr_rs, fw_ss, fw_rs, col_ss, col_rs, sib_ss, sib_rs, row_ss, row_rs,
    rg_ss, rg_rs, us_ss, us_rs, v_ss, v_rs, q_ss, q_rs,
):
    dp = lax.axis_index("dp")
    x = lax.axis_index("proto")
    z, y, c = dp // (NY * NC), (dp // NC) % NY, dp % NC

    def dev(dz, dy, flip, dx):
        core = 1 - c if flip else c
        return ((((z + dz) % NZ) * NY + (y + dy) % NY) * NC + core, (x + dx) % NX)

    right, left, sibling = dev(1, 0, 0, 0), dev(NZ - 1, 0, 0, 0), dev(0, 0, 1, 0)
    z_peers = [(o, dev(o, 0, 0, 0)) for o in range(1, NZ)]
    yx_peers = [((a, b), dev(0, a, 0, b)) for a in range(NY) for b in range(NX) if (a, b) != (0, 0)]

    def copy(src, dst, ss, rs, to):
        return pltpu.make_async_remote_copy(
            src_ref=src, dst_ref=dst, send_sem=ss, recv_sem=rs, device_id=to, device_id_type=MESH
        )

    barrier = pltpu.get_barrier_semaphore()
    for _, peer in z_peers + yx_peers:
        pl.semaphore_signal(barrier, inc=1, device_id=peer, device_id_type=MESH)
    pl.semaphore_signal(barrier, inc=1, device_id=sibling, device_id_type=MESH)

    protos[0:B, :] = unit_rows(proto_ref[...])[0].astype(bf16)
    teach[0:B, :] = unit_rows(teacher_ref[...])[0].astype(bf16)
    stud[0:B, :] = unit_rows(student_ref[...])[0].astype(bf16)
    pl.semaphore_wait(barrier, len(z_peers) + len(yx_peers) + 1)

    sent = []

    ag = {}

    def ag_step(k):
        for s in range(SUB):
            for d in (0, 1):
                if k == 3 and (2 * s) // SUB != d:
                    continue
                if k > 0:
                    ag[(k - 1, s, d)].wait_recv()
                src = (NZ - k) % NZ if d == 0 else k
                dst = NZ - k - 1 if d == 0 else k + 1
                cp = copy(
                    protos.at[pl.ds(src * B + s * PIECE, PIECE)],
                    protos.at[pl.ds(dst * B + s * PIECE, PIECE)],
                    ag_ss.at[k, s, d], ag_rs.at[k, s, d], right if d == 0 else left,
                )
                cp.start()
                ag[(k, s, d)] = cp
                sent.append(cp)

    def ag_wait(k):
        for s in range(SUB):
            for d in (0, 1):
                cp = ag.get((k, s, d))
                if cp is not None:
                    cp.wait_recv()

    cr, fw = {}, {}

    def crop_send(w, ref):
        for j in (1, 3, 2):
            t = (NY - j) % NY
            cp = copy(
                ref.at[pl.ds(0, B)], ref.at[pl.ds(2 * t * B, B)],
                cr_ss.at[w, j - 1], cr_rs.at[w, t - 1], dev(0, j, 0, 0),
            )
            cp.start()
            cr[(w, j)] = cp
            sent.append(cp)
        forward(w, ref, 0)

    def forward(w, ref, j):
        cp = copy(
            ref.at[pl.ds(2 * j * B, B)], ref.at[pl.ds((2 * j + 1) * B, B)],
            fw_ss.at[w, j], fw_rs.at[w, j], sibling,
        )
        cp.start()
        fw[(w, j)] = cp
        sent.append(cp)

    def crop_forward(w, ref):
        for j in (1, 3, 2):
            cr[(w, (NY - j) % NY)].wait_recv()
            forward(w, ref, j)

    def crop_wait(w):
        for j in range(NY):
            fw[(w, j)].wait_recv()

    lane_tiles = COLS // 128

    def teacher_slot(s):
        weights = protos[s * B:(s + 1) * B, :]

        def body(i, acc):
            rows = pl.ds(pl.multiple_of(i * TILE, TILE), TILE)
            dots = lax.dot_general(teach[rows, :], weights, NT, preferred_element_type=f32)
            values = jnp.exp2(dots * (LOG2E / teacher_temp))
            t_exp[rows, s * B:(s + 1) * B] = values
            return acc + jnp.sum(values.reshape(TILE // 8, 8, B), axis=0)

        acc = lax.fori_loop(0, ROWS // TILE, body, jnp.zeros((8, B), f32))
        col_send[0, s:s + 1, :] = jnp.sum(acc, axis=0, keepdims=True)

    def student_slot(s):
        weights = protos[s * B:(s + 1) * B, :]

        def body(i, _):
            rows = pl.ds(pl.multiple_of(i * TILE, TILE), TILE)
            dots = lax.dot_general(stud[rows, :], weights, NT, preferred_element_type=f32)
            values = jnp.exp2(dots * (LOG2E / student_temp))
            s_exp[rows, s * B:(s + 1) * B] = values
            both = values[:, :128] + values[:, 128:]
            part[rows, :] = both if s == 0 else part[rows, :] + both
            return 0

        lax.fori_loop(0, ROWS // TILE, body, 0)

    ag_step(0)
    crop_send(0, teach)
    crop_send(1, stud)
    ag_step(1)
    crop_forward(0, teach)
    ag_step(2)
    crop_wait(0)
    teacher_slot(0)
    teacher_slot(1)
    teacher_slot(7)
    ag_step(3)
    crop_forward(1, stud)
    teacher_slot(2)
    teacher_slot(6)
    for s in range(SUB):
        ag[(2, s, 1 - (2 * s) // SUB)].wait_recv()
    teacher_slot(3)
    teacher_slot(5)
    ag_wait(3)
    teacher_slot(4)
    crop_wait(1)

    def start_col(n):
        cps = []
        for o, peer in z_peers:
            t = (NZ - o) % NZ
            cp = copy(col_send.at[n], col_recv.at[n, t - 1], col_ss.at[n, o - 1], col_rs.at[n, t - 1], peer)
            cp.start()
            cps.append(cp)
        sent.extend(cps)
        return cps

    def finish_col(n, cps):
        total = col_send[n]
        for cp in cps:
            cp.wait_recv()
        for o in range(1, NZ):
            total = total + pltpu.roll(col_recv[n, o - 1], o, 0)
        return 1.0 / (PROTOS * total)

    def start_sibling(n, height):
        cp = copy(
            row_sib.at[n, pl.ds(0, height)], sib_recv.at[n, pl.ds(0, height)],
            sib_ss.at[n], sib_rs.at[n], sibling,
        )
        cp.start()
        sent.append(cp)
        return cp

    even = lax.broadcasted_iota(jnp.int32, (8, B), 0) % 2 == 0

    def swap(v):
        return jnp.where(even, pltpu.roll(v, 7, 0), pltpu.roll(v, 1, 0))

    def start_row(n, height, cp):
        cp.wait_recv()
        for h in range(0, height, 8):
            row_send[n, h:h + 8, :] = row_sib[n, h:h + 8, :] + swap(sib_recv[n, h:h + 8, :])
        cps = []
        for (a, b), peer in yx_peers:
            i, t = a * NX + b, ((NY - a) % NY) * NX + (NX - b) % NX
            cp = copy(
                row_send.at[n, pl.ds(0, height)], row_recv.at[n, t - 1, pl.ds(0, height)],
                row_ss.at[n, i - 1], row_rs.at[n, t - 1], peer,
            )
            cp.start()
            cps.append(cp)
        sent.extend(cps)
        return cps

    def finish_row(n, height, cps):
        for cp in cps:
            cp.wait_recv()
        out = []
        for h in range(0, height, 8):
            total = row_send[n, h:h + 8, :]
            for a in range(NY):
                some = None
                for b in range(NX):
                    if (a, b) == (0, 0):
                        continue
                    v = row_recv[n, a * NX + b - 1, h:h + 8, :]
                    some = v if some is None else some + v
                total = total + (some if a == 0 else pltpu.roll(some, 2 * a, 0))
            out.append(total)
        return out

    lane = lax.broadcasted_iota(jnp.int32, (B, 128), 1)

    def to_lanes(n, h):
        row_sib[n, h:h + 8, :] = jnp.transpose(mat[...])[0:8, :]

    def to_rows(v, out):
        wide = jnp.transpose(jnp.concatenate([v, jnp.zeros((120, B), f32)], axis=0))
        for q in range(8):
            out[q * B:(q + 1) * B, :] = jnp.broadcast_to(wide[:, q:q + 1], (B, 128))

    def row_pass(col):
        mat[...] = jnp.zeros((B, 128), f32)

        def body(q, _):
            rows = pl.ds(pl.multiple_of(q * B, B), B)
            acc = jnp.zeros((B, 128), f32)
            for t in range(lane_tiles):
                s, h = t // 2, t % 2
                acc = acc + t_exp[rows, t * 128:(t + 1) * 128] * col[s:s + 1, h * 128:(h + 1) * 128]
            mat[...] = jnp.where(lane == q, jnp.sum(acc, axis=1, keepdims=True), mat[...])
            return 0

        lax.fori_loop(0, 8, body, 0)

    def partition_pass():
        mat[...] = jnp.zeros((B, 128), f32)

        def body(q, _):
            rows = pl.ds(pl.multiple_of(q * B, B), B)
            mat[...] = jnp.where(lane == q, jnp.sum(part[rows, :], axis=1, keepdims=True), mat[...])
            return 0

        lax.fori_loop(0, 8, body, 0)

    def col_pass(n):
        def body(i, acc):
            rows = pl.ds(pl.multiple_of(i * 64, 64), 64)
            scale = jnp.concatenate([row_b[rows, :]] * lane_tiles, axis=1)
            values = t_exp[rows, :] * scale
            return acc + jnp.sum(values.reshape(8, 8, COLS), axis=0)

        acc = lax.fori_loop(0, ROWS // 64, body, jnp.zeros((8, COLS), f32))
        total = jnp.sum(acc, axis=0, keepdims=True)
        for s in range(NZ):
            col_send[n, s:s + 1, :] = total[:, s * B:(s + 1) * B]

    cps = start_col(0)
    for s in range(4):
        student_slot(s)
    col = finish_col(0, cps)
    row_pass(col)
    to_lanes(0, 0)
    cps = start_row(0, 8, start_sibling(0, 8))
    for s in range(4, 8):
        student_slot(s)
    (row_total,) = finish_row(0, 8, cps)
    to_rows(1.0 / (CROPS * row_total), row_b)
    col_pass(1)
    cps = start_col(1)
    partition_pass()
    to_lanes(1, 8)
    for q in range(8):
        stud_t[:, q * B:(q + 1) * B] = jnp.transpose(stud[q * B:(q + 1) * B, :].astype(f32)).astype(bf16)
    col = finish_col(1, cps)
    row_pass(col)
    to_lanes(1, 0)
    cps = start_row(1, 16, start_sibling(1, 16))
    row_total, partition = finish_row(1, 16, cps)
    to_rows(1.0 / (CROPS * row_total), row_b)
    col_pass(2)
    cps = start_col(2)
    to_rows((loss_scale / student_temp) / partition, row_a)
    col = finish_col(2, cps)
    row_pass(col)
    to_lanes(2, 0)
    cps = start_row(2, 8, start_sibling(2, 8))
    (row_total,) = finish_row(2, 8, cps)
    to_rows((loss_scale / student_temp) / row_total, row_b)

    def grad_slot(s):
        cols = slice(s * B, (s + 1) * B)

        def body(i, _):
            rows = pl.ds(pl.multiple_of(i * B, B), B)
            a = row_a[rows, :]
            b = row_b[rows, :]
            for h in range(2):
                at = slice(s * B + h * 128, s * B + (h + 1) * 128)
                scale = col[s:s + 1, h * 128:(h + 1) * 128]
                grad[rows, at] = (s_exp[rows, at] * a - t_exp[rows, at] * b * scale).astype(bf16)
            return 0

        lax.fori_loop(0, ROWS // B, body, 0)
        chunk[s] = jnp.dot(stud_t[...], grad[:, cols], preferred_element_type=f32)

    rg = {}
    H = B // 2

    def ring(m, d, h):
        s = 4 - m if d == 0 else 4 + m
        rows = slice(h * H, (h + 1) * H)
        value = chunk[s, rows, :]
        if (m - 1, d, h) in rg:
            rg[(m - 1, d, h)].wait_recv()
            value = value + ring_recv[m - 1, d, rows, :].astype(f32)
        ring_send[m, d, rows, :] = value.astype(bf16)
        cp = copy(
            ring_send.at[m, d, pl.ds(h * H, H)], ring_recv.at[m, d, pl.ds(h * H, H)],
            rg_ss.at[m, d, h], rg_rs.at[m, d, h], right if d == 0 else left,
        )
        cp.start()
        rg[(m, d, h)] = cp
        sent.append(cp)

    def u_block(q):
        return jnp.dot(grad[q * B:(q + 1) * B, :], protos[...], preferred_element_type=f32)

    grad_slot(4)
    ring(0, 0, 0)
    ring(0, 1, 1)
    grad_slot(3)
    ring(1, 0, 1)
    grad_slot(5)
    ring(1, 1, 0)
    grad_slot(2)
    grad_slot(6)
    ring(1, 0, 0)
    ring(1, 1, 1)
    grad_slot(1)
    grad_slot(7)
    ring(2, 0, 1)
    ring(2, 1, 0)
    grad_slot(0)
    us = []
    for j in range(NY):
        u_send[j] = u_block(2 * j + 1).astype(bf16)
        cp = copy(u_send.at[j], u_sib.at[j], us_ss.at[j], us_rs.at[j], sibling)
        cp.start()
        us.append(cp)
    sent.extend(us)
    ring(2, 0, 0)
    ring(2, 1, 1)
    for j in range(NY):
        u_ref[j] = u_block(2 * j)
    for j in range(NY):
        us[j].wait_recv()
        total = u_ref[j] + u_sib[j].astype(f32)
        u_ref[j] = total
        v_send[j] = total.astype(bf16)
    Q = B // NX
    vs = []
    for (a, b), peer in yx_peers:
        i, t = a * NX + b, ((NY - a) % NY) * NX + (NX - b) % NX
        at = pl.multiple_of(((x + b) % NX) * Q, Q)
        cp = copy(v_send.at[a, pl.ds(at, Q)], v_recv.at[t - 1], v_ss.at[i - 1], v_rs.at[t - 1], peer)
        cp.start()
        vs.append(cp)
    sent.extend(vs)
    ring(3, 0, 1)
    ring(3, 1, 0)
    ring(3, 0, 0)
    ring(3, 1, 1)

    mine = pl.ds(pl.multiple_of(x * Q, Q), Q)
    for cp in vs:
        cp.wait_recv()
    total = u_ref[0, mine, :]
    for i in range(NY * NX - 1):
        total = total + v_recv[i].astype(f32)
    unit, inverse = unit_rows(student_ref[mine, :])
    q_send[...] = inverse * (total - unit * jnp.sum(unit * total, axis=1, keepdims=True))
    qs = []
    for b in range(1, NX):
        t = NX - b
        cp = copy(q_send, q_full.at[pl.ds(pl.multiple_of(x * Q, Q), Q)], q_ss.at[b - 1], q_rs.at[t - 1], dev(0, 0, 0, b))
        cp.start()
        qs.append(cp)
    sent.extend(qs)

    for key in ((3, 0, 1), (3, 1, 0), (3, 0, 0), (3, 1, 1)):
        rg[key].wait_recv()
    total = chunk[0] + ring_recv[3, 0].astype(f32) + ring_recv[3, 1].astype(f32)
    total = jnp.transpose(total)
    unit, inverse = unit_rows(proto_ref[...])
    gp_ref[...] = inverse * (total - unit * jnp.sum(unit * total, axis=1, keepdims=True))

    for cp in qs:
        cp.wait_recv()
    gs_ref[...] = q_full[...]
    gs_ref[mine, :] = q_send[...]
    for cp in sent:
        cp.wait_send()


def shards(student_feat, teacher_feat, prototypes):
    vmem = pltpu.VMEM
    dma = pltpu.SemaphoreType.DMA
    n_yx = NY * NX - 1
    pairs = [
        dma((4, SUB, 2)), dma((2, NY - 1)), dma((2, NY)), dma((SWEEPS, NZ - 1)), dma((SWEEPS,)),
        dma((SWEEPS, n_yx)), dma((4, 2, 2)), dma((NY,)), dma((n_yx,)), dma((NX - 1,)),
    ]
    return pl.pallas_call(
        kernel,
        out_shape=[jax.ShapeDtypeStruct((B, B), f32), jax.ShapeDtypeStruct((B, B), f32)],
        in_specs=[pl.BlockSpec(memory_space=pltpu.VMEM)] * 3,
        out_specs=[pl.BlockSpec(memory_space=pltpu.VMEM)] * 2,
        scratch_shapes=[
            vmem((COLS, B), bf16),
            vmem((ROWS, B), bf16),
            vmem((ROWS, B), bf16),
            vmem((B, ROWS), bf16),
            vmem((ROWS, COLS), f32),
            vmem((ROWS, COLS), f32),
            vmem((ROWS, COLS), bf16),
            vmem((ROWS, 128), f32),
            vmem((ROWS, 128), f32),
            vmem((ROWS, 128), f32),
            vmem((B, 128), f32),
            vmem((SWEEPS, 8, B), f32),
            vmem((SWEEPS, NZ - 1, 8, B), f32),
            vmem((SWEEPS, 16, B), f32),
            vmem((SWEEPS, 16, B), f32),
            vmem((SWEEPS, 16, B), f32),
            vmem((SWEEPS, n_yx, 16, B), f32),
            vmem((NZ, B, B), f32),
            vmem((4, 2, B, B), bf16),
            vmem((4, 2, B, B), bf16),
            vmem((NY, B, B), f32),
            vmem((NY, B, B), bf16),
            vmem((NY, B, B), bf16),
            vmem((NY, B, B), bf16),
            vmem((n_yx, B // NX, B), bf16),
            vmem((B // NX, B), f32),
            vmem((B, B), f32),
        ] + [s for s in pairs for _ in range(2)],
        compiler_params=pltpu.CompilerParams(
            collective_id=0, has_side_effects=True, vmem_limit_bytes=63 * 2**20
        ),
    )(student_feat, teacher_feat, prototypes)


def solution(mesh):
    in_specs = (P("dp", None), P("dp", None), P(("dp", "proto"), None))
    out_specs = (P("dp", None), P(("dp", "proto"), None))
    return jax.shard_map(shards, mesh=mesh, in_specs=in_specs, out_specs=out_specs, check_vma=False)
```

```python
import math

import jax
import jax.numpy as jnp
from jax import lax
from jax.experimental import pallas as pl
from jax.experimental.pallas import tpu as pltpu
from jax.sharding import PartitionSpec as P

NZ, NY, NX, NC = 8, 4, 4, 2
B = 256
ROWS = NY * NC * B
COLS = NZ * B
CROPS = 16384
PROTOS = 65536
SWEEPS = 3
teacher_temp = 0.07
student_temp = 0.1
loss_scale = 1024.0
epsilon = 1e-06
LOG2E = math.log2(math.e)
MESH = pl.DeviceIdType.MESH
NT = (((1,), (1,)), ((), ()))
f32 = jnp.float32
bf16 = jnp.bfloat16
SUB = 4
PIECE = B // SUB
H = B // 2
N_YX = NY * NX - 1
OFFSET = (0, 8, 24, 32)
AG, CROP, FORWARD, COL, SIB, ROW, RING, US, V, QS, GROUPS = 0, 1, 3, 5, 6, 7, 8, 9, 10, 11, 12


def unit_rows(matrix):
    values = matrix.astype(f32)
    inverse = lax.rsqrt(jnp.sum(values * values, axis=-1, keepdims=True) + epsilon)
    return values * inverse, inverse


def kernel(
    student_ref, teacher_ref, proto_ref, gs_ref, gp_ref,
    protos, teach, stud, stud_t, t_exp, s_exp, grad, part, row_a, row_b, mat,
    col_send, col_recv, row_sib, row_send, sib_recv, row_recv,
    chunk, ring_send, ring_recv, u_ref, u_send, u_sib, v_send, v_recv, q_full,
    ss, ag_rs, hop_rs, far_rs, fw_rs, col_rs, sib_rs, row_rs, rg_rs, us_rs, vq_rs,
):
    dp = lax.axis_index("dp")
    x = lax.axis_index("proto")
    z, y, c = dp // (NY * NC), (dp // NC) % NY, dp % NC

    def dev(dz, dy, flip, dx):
        core = 1 - c if flip else c
        return ((((z + dz) % NZ) * NY + (y + dy) % NY) * NC + core, (x + dx) % NX)

    right, left, sibling = dev(1, 0, 0, 0), dev(NZ - 1, 0, 0, 0), dev(0, 0, 1, 0)
    up, down = dev(0, 1, 0, 0), dev(0, NY - 1, 0, 0)
    z_peers = [(o, dev(o, 0, 0, 0)) for o in (4, 3, 5, 2, 6, 1, 7)]
    far = sorted(
        ((a, b) for a in range(NY) for b in range(NX) if (a, b) != (0, 0)),
        key=lambda ab: -min(ab[0], NY - ab[0]) - min(ab[1], NX - ab[1]),
    )
    yx_peers = [((a, b), dev(0, a, 0, b)) for a, b in far]

    def copy(src, dst, group, rs, to):
        return pltpu.make_async_remote_copy(
            src_ref=src, dst_ref=dst, send_sem=ss.at[group], recv_sem=rs, device_id=to, device_id_type=MESH
        )

    def wait_recv(ref, rs):
        copy(ref, ref, 0, rs, right).wait_recv()

    def wait_send(ref, group):
        copy(ref, ref, group, vq_rs.at[0], right).wait_send()

    barrier = pltpu.get_barrier_semaphore()
    near = [right, left, up, down, sibling] + [dev(0, 0, 0, b) for b in (2, 1, 3)]
    for peer in near:
        pl.semaphore_signal(barrier, inc=1, device_id=peer, device_id_type=MESH)

    protos[0:B, :] = unit_rows(proto_ref[...])[0].astype(bf16)
    teach[0:B, :] = unit_rows(teacher_ref[...])[0].astype(bf16)
    stud[0:B, :] = unit_rows(student_ref[...])[0].astype(bf16)
    pl.semaphore_wait(barrier, len(near))

    ag = {}

    def ag_step(k):
        for s in range(SUB):
            for d in (0, 1):
                if k == 3 and (2 * s) // SUB != d:
                    continue
                if k > 0:
                    ag[(k - 1, s, d)].wait_recv()
                src = (NZ - k) % NZ if d == 0 else k
                dst = NZ - k - 1 if d == 0 else k + 1
                cp = copy(
                    protos.at[pl.ds(src * B + s * PIECE, PIECE)],
                    protos.at[pl.ds(dst * B + s * PIECE, PIECE)],
                    AG, ag_rs.at[k, s, d], right if d == 0 else left,
                )
                cp.start()
                ag[(k, s, d)] = cp

    def ag_wait(k):
        for s in range(SUB):
            for d in (0, 1):
                cp = ag.get((k, s, d))
                if cp is not None:
                    cp.wait_recv()

    hop, last = {}, {}
    crops = (teach, stud)

    def forward(w, j):
        ref = crops[w]
        copy(
            ref.at[pl.ds(2 * j * B, B)], ref.at[pl.ds((2 * j + 1) * B, B)], FORWARD + w, fw_rs.at[w], sibling
        ).start()

    def crop_start(w):
        ref = crops[w]
        for first in (0, 1):
            for d, to, j in ((0, up, 3), (1, down, 1)):
                h = first if d == 0 else 1 - first
                cp = copy(
                    ref.at[pl.ds(h * H, H)], ref.at[pl.ds(2 * j * B + h * H, H)],
                    CROP + w, hop_rs.at[w, d, h], to,
                )
                cp.start()
                hop[(w, d, h)] = cp
        forward(w, 0)

    def crop_relay(w):
        ref = crops[w]
        for d, to, j in ((0, up, 3), (1, down, 1)):
            hop[(w, d, d)].wait_recv()
            cp = copy(
                ref.at[pl.ds(2 * j * B + d * H, H)], ref.at[pl.ds(4 * B + d * H, H)],
                CROP + w, far_rs.at[w, d], to,
            )
            cp.start()
            last[(w, d)] = cp
        for d, j in ((0, 3), (1, 1)):
            hop[(w, d, 1 - d)].wait_recv()
            forward(w, j)

    def crop_last(w):
        for d in (0, 1):
            last[(w, d)].wait_recv()
        forward(w, 2)

    def crop_wait(w):
        wait_recv(crops[w].at[pl.ds(0, NY * B)], fw_rs.at[w])

    lane_tiles = COLS // 128

    def teacher_slot(s):
        cols = slice(s * B, (s + 1) * B)
        dots = lax.dot_general(teach[...], protos[cols, :], NT, preferred_element_type=f32)
        values = jnp.exp2(dots * (LOG2E / teacher_temp))
        t_exp[:, cols] = values
        col_send[0, s:s + 1, :] = jnp.sum(values, axis=0, keepdims=True)

    def student_slot(s):
        cols = slice(s * B, (s + 1) * B)
        dots = lax.dot_general(stud[...], protos[cols, :], NT, preferred_element_type=f32)
        values = jnp.exp2(dots * (LOG2E / student_temp))
        s_exp[:, cols] = values
        both = values[:, :128] + values[:, 128:]
        part[...] = both if s == 0 else part[...] + both

    ag_step(0)
    crop_start(0)
    crop_start(1)
    ag_step(1)
    crop_relay(0)
    ag_step(2)
    crop_last(0)
    crop_relay(1)
    ag_step(3)
    crop_wait(0)
    for s in (0, 1, 7, 2, 6):
        teacher_slot(s)
    for s in range(SUB):
        ag[(2, s, 1 - (2 * s) // SUB)].wait_recv()
    teacher_slot(3)
    teacher_slot(5)
    ag_wait(3)
    teacher_slot(4)

    def start_col(n):
        for o, peer in z_peers:
            copy(col_send.at[n], col_recv.at[n, NZ - o - 1], COL, col_rs.at[n], peer).start()

    def finish_col(n):
        total = col_send[n]
        wait_recv(col_recv.at[n], col_rs.at[n])
        for o in range(1, NZ):
            total = total + pltpu.roll(col_recv[n, o - 1], o, 0)
        return 1.0 / (PROTOS * total)

    def start_sibling(n):
        at = pl.ds(OFFSET[n], OFFSET[n + 1] - OFFSET[n])
        copy(row_sib.at[at], sib_recv.at[at], SIB, sib_rs.at[n], sibling).start()

    even = lax.broadcasted_iota(jnp.int32, (8, B), 0) % 2 == 0

    def swap(v):
        return jnp.where(even, pltpu.roll(v, 7, 0), pltpu.roll(v, 1, 0))

    def start_row(n):
        start, height = OFFSET[n], OFFSET[n + 1] - OFFSET[n]
        at = pl.ds(start, height)
        wait_recv(sib_recv.at[at], sib_rs.at[n])
        for h in range(start, start + height, 8):
            row_send[h:h + 8, :] = row_sib[h:h + 8, :] + swap(sib_recv[h:h + 8, :])
        for (a, b), peer in yx_peers:
            t = ((NY - a) % NY) * NX + (NX - b) % NX - 1
            to = row_recv.at[pl.ds(N_YX * start + t * height, height)]
            copy(row_send.at[at], to, ROW, row_rs.at[n], peer).start()

    def finish_row(n):
        start, height = OFFSET[n], OFFSET[n + 1] - OFFSET[n]
        wait_recv(row_recv.at[pl.ds(N_YX * start, N_YX * height)], row_rs.at[n])
        out = []
        for h in range(0, height, 8):
            total = row_send[start + h:start + h + 8, :]
            for a in range(NY):
                some = None
                for b in range(NX):
                    if (a, b) == (0, 0):
                        continue
                    k = N_YX * start + (a * NX + b - 1) * height + h
                    v = row_recv[k:k + 8, :]
                    some = v if some is None else some + v
                total = total + (some if a == 0 else pltpu.roll(some, 2 * a, 0))
            out.append(total)
        return out

    lane = lax.broadcasted_iota(jnp.int32, (B, 128), 1)

    def to_lanes(at):
        row_sib[at:at + 8, :] = jnp.transpose(mat[...])[0:8, :]

    def to_rows(v, out):
        wide = jnp.transpose(jnp.concatenate([v, jnp.zeros((120, B), f32)], axis=0))
        for q in range(8):
            out[q * B:(q + 1) * B, :] = jnp.broadcast_to(wide[:, q:q + 1], (B, 128))

    def row_pass(col):
        mat[...] = jnp.zeros((B, 128), f32)

        def body(q, _):
            rows = pl.ds(pl.multiple_of(q * B, B), B)
            acc = jnp.zeros((B, 128), f32)
            for t in range(lane_tiles):
                s, h = t // 2, t % 2
                acc = acc + t_exp[rows, t * 128:(t + 1) * 128] * col[s:s + 1, h * 128:(h + 1) * 128]
            mat[...] = jnp.where(lane == q, jnp.sum(acc, axis=1, keepdims=True), mat[...])
            return 0

        lax.fori_loop(0, 8, body, 0)

    def partition_pass():
        mat[...] = jnp.zeros((B, 128), f32)

        def body(q, _):
            rows = pl.ds(pl.multiple_of(q * B, B), B)
            mat[...] = jnp.where(lane == q, jnp.sum(part[rows, :], axis=1, keepdims=True), mat[...])
            return 0

        lax.fori_loop(0, 8, body, 0)

    def col_pass(n):
        def body(i, acc):
            rows = pl.ds(pl.multiple_of(i * 64, 64), 64)
            scale = jnp.concatenate([row_b[rows, :]] * lane_tiles, axis=1)
            values = t_exp[rows, :] * scale
            return acc + jnp.sum(values.reshape(8, 8, COLS), axis=0)

        acc = lax.fori_loop(0, ROWS // 64, body, jnp.zeros((8, COLS), f32))
        total = jnp.sum(acc, axis=0, keepdims=True)
        for s in range(NZ):
            col_send[n, s:s + 1, :] = total[:, s * B:(s + 1) * B]

    start_col(0)
    crop_last(1)
    crop_wait(1)
    for s in range(4):
        student_slot(s)
    row_pass(finish_col(0))
    to_lanes(OFFSET[0])
    start_sibling(0)
    start_row(0)
    for s in range(4, 8):
        student_slot(s)
    (row_total,) = finish_row(0)
    to_rows(1.0 / (CROPS * row_total), row_b)
    col_pass(1)
    start_col(1)
    partition_pass()
    to_lanes(OFFSET[1] + 8)
    for q in range(8):
        stud_t[:, q * B:(q + 1) * B] = jnp.transpose(stud[q * B:(q + 1) * B, :].astype(f32)).astype(bf16)
    row_pass(finish_col(1))
    to_lanes(OFFSET[1])
    start_sibling(1)
    start_row(1)
    row_total, partition = finish_row(1)
    to_rows(1.0 / (CROPS * row_total), row_b)
    col_pass(2)
    start_col(2)
    to_rows((loss_scale / student_temp) / partition, row_a)
    col = finish_col(2)
    row_pass(col)
    to_lanes(OFFSET[2])
    start_sibling(2)
    start_row(2)
    (row_total,) = finish_row(2)
    to_rows((loss_scale / student_temp) / row_total, row_b)

    def grad_part(start, height, slots):
        for r in range(start, start + height, 16):
            rows = slice(r, r + 16)
            a = row_a[rows, :]
            b = row_b[rows, :]
            for s in slots:
                for h in range(2):
                    at = slice(s * B + h * 128, s * B + (h + 1) * 128)
                    scale = col[s:s + 1, h * 128:(h + 1) * 128]
                    grad[rows, at] = (s_exp[rows, at] * a - t_exp[rows, at] * b * scale).astype(bf16)

    def chunk_dot(s):
        chunk[s] = jnp.dot(stud_t[...], grad[:, s * B:(s + 1) * B], preferred_element_type=f32)

    rg = {}

    def ring(m, d, pieces):
        s = 4 - m if d == 0 else 4 + m
        for p in pieces:
            rows = slice(p * PIECE, (p + 1) * PIECE)
            value = chunk[s, rows, :]
            if (m - 1, d, p) in rg:
                rg[(m - 1, d, p)].wait_recv()
                value = value + ring_recv[2 * (m - 1) + d, rows, :].astype(f32)
            ring_send[2 * m + d, rows, :] = value.astype(bf16)
            at = pl.ds(p * PIECE, PIECE)
            cp = copy(
                ring_send.at[2 * m + d, at], ring_recv.at[2 * m + d, at],
                RING, rg_rs.at[m, d, p], right if d == 0 else left,
            )
            cp.start()
            rg[(m, d, p)] = cp

    low, high = range(SUB // 2), range(SUB // 2, SUB)

    def u_dot(q):
        return jnp.dot(grad[q * B:(q + 1) * B, :], protos[...], preferred_element_type=f32)

    us = {}

    def u_pair(j, slots):
        grad_part((2 * j + 1) * B, B, slots)
        grad_part(2 * j * B, B, slots)
        u_send[j] = u_dot(2 * j + 1).astype(bf16)
        cp = copy(u_send.at[j], u_sib.at[j], US, us_rs.at[j], sibling)
        cp.start()
        us[j] = cp
        u_ref[j] = u_dot(2 * j)

    Q = B // NX
    mine = pl.ds(pl.multiple_of(x * Q, Q), Q)

    def v_start(j):
        us[j].wait_recv()
        total = u_ref[j] + u_sib[j].astype(f32)
        if j == 0:
            u_ref[j] = total
        v_send[j] = total.astype(bf16)
        for b in (2, 1, 3, 0):
            if (j, b) == (0, 0):
                continue
            t = ((NY - j) % NY) * NX + (NX - b) % NX - 1
            at = pl.multiple_of(((x + b) % NX) * Q, Q)
            copy(v_send.at[j, pl.ds(at, Q)], v_recv.at[t], V, vq_rs.at[0], dev(0, j, 0, b)).start()

    grad_part(0, ROWS, (4,))
    chunk_dot(4)
    ring(0, 0, low)
    ring(0, 1, high)
    grad_part(0, ROWS, (3, 5))
    chunk_dot(3)
    ring(1, 0, high)
    chunk_dot(5)
    ring(1, 1, low)
    rest = (0, 1, 2, 6, 7)
    u_pair(2, rest)
    u_pair(1, rest)
    ring(1, 0, low)
    ring(1, 1, high)
    v_start(2)
    u_pair(3, rest)
    v_start(1)
    u_pair(0, rest)
    v_start(3)
    chunk_dot(2)
    ring(2, 0, high)
    chunk_dot(6)
    ring(2, 1, low)
    v_start(0)
    ring(2, 0, low)
    ring(2, 1, high)
    chunk_dot(1)
    ring(3, 0, high)
    chunk_dot(7)
    ring(3, 1, low)
    chunk_dot(0)
    ring(3, 0, low)
    ring(3, 1, high)

    wait_recv(v_recv, vq_rs.at[0])
    total = u_ref[0, mine, :]
    for i in range(N_YX):
        total = total + v_recv[i].astype(f32)
    unit, inverse = unit_rows(student_ref[mine, :])
    q_full[mine, :] = (inverse * (total - unit * jnp.sum(unit * total, axis=1, keepdims=True))).astype(bf16)
    for b in (2, 1, 3):
        copy(q_full.at[mine], q_full.at[mine], QS, vq_rs.at[1], dev(0, 0, 0, b)).start()

    for m, d, p in rg:
        if m == 3:
            rg[(m, d, p)].wait_recv()
    total = chunk[0] + ring_recv[6].astype(f32) + ring_recv[7].astype(f32)
    total = jnp.transpose(total)
    unit, inverse = unit_rows(proto_ref[...])
    gp_ref[...] = inverse * (total - unit * jnp.sum(unit * total, axis=1, keepdims=True))

    wait_recv(q_full.at[pl.ds(0, (NX - 1) * Q)], vq_rs.at[1])
    gs_ref[...] = q_full[...].astype(f32)

    wait_send(protos.at[pl.ds(0, 7 * B)], AG)
    for w in (0, 1):
        wait_send(crops[w].at[pl.ds(0, 3 * B)], CROP + w)
        wait_send(crops[w].at[pl.ds(0, 4 * B)], FORWARD + w)
    wait_send(col_recv, COL)
    wait_send(row_sib, SIB)
    wait_send(row_recv, ROW)
    wait_send(ring_recv.at[pl.ds(0, 7)], RING)
    wait_send(u_sib, US)
    wait_send(v_recv, V)
    wait_send(q_full.at[pl.ds(0, (NX - 1) * Q)], QS)


def shards(student_feat, teacher_feat, prototypes):
    vmem = pltpu.VMEM
    dma = pltpu.SemaphoreType.DMA
    sems = [
        dma((GROUPS,)), dma((4, SUB, 2)), dma((2, 2, 2)), dma((2, 2)), dma((2,)), dma((SWEEPS,)), dma((SWEEPS,)),
        dma((SWEEPS,)), dma((4, 2, SUB)), dma((NY,)), dma((2,)),
    ]
    return pl.pallas_call(
        kernel,
        out_shape=[jax.ShapeDtypeStruct((B, B), f32), jax.ShapeDtypeStruct((B, B), f32)],
        in_specs=[pl.BlockSpec(memory_space=pltpu.VMEM)] * 3,
        out_specs=[pl.BlockSpec(memory_space=pltpu.VMEM)] * 2,
        scratch_shapes=[
            vmem((COLS, B), bf16),
            vmem((ROWS, B), bf16),
            vmem((ROWS, B), bf16),
            vmem((B, ROWS), bf16),
            vmem((ROWS, COLS), f32),
            vmem((ROWS, COLS), f32),
            vmem((ROWS, COLS), bf16),
            vmem((ROWS, 128), f32),
            vmem((ROWS, 128), f32),
            vmem((ROWS, 128), f32),
            vmem((B, 128), f32),
            vmem((SWEEPS, 8, B), f32),
            vmem((SWEEPS, NZ - 1, 8, B), f32),
            vmem((OFFSET[-1], B), f32),
            vmem((OFFSET[-1], B), f32),
            vmem((OFFSET[-1], B), f32),
            vmem((N_YX * OFFSET[-1], B), f32),
            vmem((NZ, B, B), f32),
            vmem((8, B, B), bf16),
            vmem((8, B, B), bf16),
            vmem((NY, B, B), f32),
            vmem((NY, B, B), bf16),
            vmem((NY, B, B), bf16),
            vmem((NY, B, B), bf16),
            vmem((N_YX, B // NX, B), bf16),
            vmem((B, B), bf16),
        ] + sems,
        compiler_params=pltpu.CompilerParams(
            collective_id=0, has_side_effects=True, vmem_limit_bytes=63 * 2**20
        ),
    )(student_feat, teacher_feat, prototypes)


def solution(mesh):
    in_specs = (P("dp", None), P("dp", None), P(("dp", "proto"), None))
    out_specs = (P("dp", None), P(("dp", "proto"), None))
    return jax.shard_map(shards, mesh=mesh, in_specs=in_specs, out_specs=out_specs, check_vma=False)
```

```python
import math

import jax
import jax.numpy as jnp
from jax import lax
from jax.experimental import pallas as pl
from jax.experimental.pallas import tpu as pltpu
from jax.sharding import PartitionSpec as P

NZ, NY, NX, NC = 8, 4, 4, 2
B = 256
ROWS = NY * NC * B
COLS = NZ * B
CROPS = 16384
PROTOS = 65536
SWEEPS = 3
teacher_temp = 0.07
student_temp = 0.1
loss_scale = 1024.0
epsilon = 1e-06
LOG2E = math.log2(math.e)
MESH = pl.DeviceIdType.MESH
NT = (((1,), (1,)), ((), ()))
f32 = jnp.float32
bf16 = jnp.bfloat16
SUB = 4
PIECE = B // SUB
H = B // 2
N_YX = NY * NX - 1
OFFSET = (0, 8, 24, 32)
AG, CROP, FORWARD, COL, SIB, ROW, RING, US, V, QS, GROUPS = 0, 1, 3, 5, 6, 7, 8, 9, 10, 11, 12


def unit_rows(matrix):
    values = matrix.astype(f32)
    inverse = lax.rsqrt(jnp.sum(values * values, axis=-1, keepdims=True) + epsilon)
    return values * inverse, inverse


def kernel(
    student_ref, teacher_ref, proto_ref, gs_ref, gp_ref,
    protos, teach, stud, stud_t, t_exp, s_exp, grad, part, row_a, row_b, mat,
    col_send, col_recv, row_sib, row_send, sib_recv, row_recv,
    chunk, ring_send, ring_recv, u_ref, u_send, u_sib, v_send, v_recv, q_full,
    ss, ag_rs, far_ag_rs, hop_rs, far_rs, fw_rs, col_rs, sib_rs, row_rs, rg_rs, us_rs, vq_rs,
):
    dp = lax.axis_index("dp")
    x = lax.axis_index("proto")
    z, y, c = dp // (NY * NC), (dp // NC) % NY, dp % NC

    def dev(dz, dy, flip, dx):
        core = 1 - c if flip else c
        return ((((z + dz) % NZ) * NY + (y + dy) % NY) * NC + core, (x + dx) % NX)

    right, left, sibling = dev(1, 0, 0, 0), dev(NZ - 1, 0, 0, 0), dev(0, 0, 1, 0)
    right2, left2 = dev(2, 0, 0, 0), dev(NZ - 2, 0, 0, 0)
    up, down = dev(0, 1, 0, 0), dev(0, NY - 1, 0, 0)
    z_peers = [(o, dev(o, 0, 0, 0)) for o in (4, 3, 5, 2, 6, 1, 7)]
    far = sorted(
        ((a, b) for a in range(NY) for b in range(NX) if (a, b) != (0, 0)),
        key=lambda ab: -min(ab[0], NY - ab[0]) - min(ab[1], NX - ab[1]),
    )
    yx_peers = [((a, b), dev(0, a, 0, b)) for a, b in far]

    def copy(src, dst, group, rs, to):
        return pltpu.make_async_remote_copy(
            src_ref=src, dst_ref=dst, send_sem=ss.at[group], recv_sem=rs, device_id=to, device_id_type=MESH
        )

    def wait_recv(ref, rs):
        copy(ref, ref, 0, rs, right).wait_recv()

    def wait_send(ref, group):
        copy(ref, ref, group, vq_rs.at[0], right).wait_send()

    barrier = pltpu.get_barrier_semaphore()
    near = [right2, left2, right, left, up, down, sibling] + [dev(0, 0, 0, b) for b in (2, 1, 3)]
    for peer in near:
        pl.semaphore_signal(barrier, inc=1, device_id=peer, device_id_type=MESH)

    protos[0:B, :] = unit_rows(proto_ref[...])[0].astype(bf16)
    teach[0:B, :] = unit_rows(teacher_ref[...])[0].astype(bf16)
    stud[0:B, :] = unit_rows(student_ref[...])[0].astype(bf16)
    pl.semaphore_wait(barrier, len(near))

    low, high = tuple(range(SUB // 2)), tuple(range(SUB // 2, SUB))
    every = low + high
    ways = ((0, right, right2, low, high), (1, left, left2, high, low))

    def block(k, d, p):
        slot = (NZ - k) % NZ if d == 0 else k
        return protos.at[pl.ds(slot * B + p * PIECE, PIECE)]

    def ag_step(k):
        for i in range(SUB):
            for d, to1, to2, first, then in ways:
                p = (first + then)[i]
                if k > 0:
                    wait_recv(block(k, d, p), ag_rs.at[k - 1, d, p])
                if k == 2 and p in first:
                    copy(block(2, d, p), block(4, d, p), AG, far_ag_rs.at[d], to2).start()
                copy(block(k, d, p), block(k + 1, d, p), AG, ag_rs.at[k, d, p], to1).start()

    def ag_wait():
        for d in (0, 1):
            for p in every:
                wait_recv(block(3, d, p), ag_rs.at[2, d, p])

    def ag_wait_far():
        for d in (0, 1):
            wait_recv(protos.at[pl.ds(0, H)], far_ag_rs.at[d])

    hop, last = {}, {}
    crops = (teach, stud)

    def forward(w, j):
        ref = crops[w]
        copy(
            ref.at[pl.ds(2 * j * B, B)], ref.at[pl.ds((2 * j + 1) * B, B)], FORWARD + w, fw_rs.at[w], sibling
        ).start()

    def crop_start(w):
        ref = crops[w]
        for first in (0, 1):
            for d, to, j in ((0, up, 3), (1, down, 1)):
                h = first if d == 0 else 1 - first
                cp = copy(
                    ref.at[pl.ds(h * H, H)], ref.at[pl.ds(2 * j * B + h * H, H)],
                    CROP + w, hop_rs.at[w, d, h], to,
                )
                cp.start()
                hop[(w, d, h)] = cp
        forward(w, 0)

    def crop_relay(w):
        ref = crops[w]
        for d, to, j in ((0, up, 3), (1, down, 1)):
            hop[(w, d, d)].wait_recv()
            cp = copy(
                ref.at[pl.ds(2 * j * B + d * H, H)], ref.at[pl.ds(4 * B + d * H, H)],
                CROP + w, far_rs.at[w, d], to,
            )
            cp.start()
            last[(w, d)] = cp
        for d, j in ((0, 3), (1, 1)):
            hop[(w, d, 1 - d)].wait_recv()
            forward(w, j)

    def crop_last(w):
        for d in (0, 1):
            last[(w, d)].wait_recv()
        forward(w, 2)

    def crop_wait(w):
        wait_recv(crops[w].at[pl.ds(0, NY * B)], fw_rs.at[w])

    def teacher_slot(s):
        cols = slice(s * B, (s + 1) * B)
        dots = lax.dot_general(teach[...], protos[cols, :], NT, preferred_element_type=f32)
        values = jnp.exp2(dots * (LOG2E / teacher_temp))
        t_exp[:, cols] = values
        total = jnp.sum(values, axis=0, keepdims=True)
        for h in (0, 1):
            col_send[0, h, s:s + 1, :] = total[:, h * 128:(h + 1) * 128]

    def student_slot(s):
        cols = slice(s * B, (s + 1) * B)
        dots = lax.dot_general(stud[...], protos[cols, :], NT, preferred_element_type=f32)
        values = jnp.exp2(dots * (LOG2E / student_temp))
        s_exp[:, cols] = values
        both = values[:, :128] + values[:, 128:]
        part[...] = both if s == 0 else part[...] + both

    ag_step(0)
    crop_start(0)
    crop_start(1)
    ag_step(1)
    crop_relay(0)
    ag_step(2)
    crop_last(0)
    crop_wait(0)
    for s in (0, 1, 7, 2, 6):
        teacher_slot(s)
    crop_relay(1)
    ag_wait()
    teacher_slot(3)
    teacher_slot(5)
    ag_wait_far()
    teacher_slot(4)

    def tile(s, h):
        return slice(s * B + h * 128, s * B + (h + 1) * 128)

    def start_col(n, h):
        for o, peer in z_peers:
            copy(col_send.at[n, h], col_recv.at[n, h, NZ - o - 1], COL, col_rs.at[n, h], peer).start()

    def finish_col(n, h):
        total = col_send[n, h]
        wait_recv(col_recv.at[n, h], col_rs.at[n, h])
        for o in range(1, NZ):
            total = total + pltpu.roll(col_recv[n, h, o - 1], o, 0)
        return 1.0 / (PROTOS * total)

    def start_sibling(n, g):
        at = pl.ds(OFFSET[n], OFFSET[n + 1] - OFFSET[n])
        copy(row_sib.at[g, at], sib_recv.at[g, at], SIB, sib_rs.at[n, g], sibling).start()

    even = lax.broadcasted_iota(jnp.int32, (8, 128), 0) % 2 == 0

    def swap(v):
        return jnp.where(even, pltpu.roll(v, 7, 0), pltpu.roll(v, 1, 0))

    def start_row(n, g):
        start, height = OFFSET[n], OFFSET[n + 1] - OFFSET[n]
        at = pl.ds(start, height)
        wait_recv(sib_recv.at[g, at], sib_rs.at[n, g])
        for i in range(start, start + height, 8):
            row_send[g, i:i + 8, :] = row_sib[g, i:i + 8, :] + swap(sib_recv[g, i:i + 8, :])
        for (a, b), peer in yx_peers:
            t = ((NY - a) % NY) * NX + (NX - b) % NX - 1
            to = row_recv.at[g, pl.ds(N_YX * start + t * height, height)]
            copy(row_send.at[g, at], to, ROW, row_rs.at[n, g], peer).start()

    def finish_row(n, g):
        start, height = OFFSET[n], OFFSET[n + 1] - OFFSET[n]
        wait_recv(row_recv.at[g, pl.ds(N_YX * start, N_YX * height)], row_rs.at[n, g])
        out = []
        for i in range(0, height, 8):
            total = row_send[g, start + i:start + i + 8, :]
            for a in range(NY):
                some = None
                for b in range(NX):
                    if (a, b) == (0, 0):
                        continue
                    k = N_YX * start + (a * NX + b - 1) * height + i
                    v = row_recv[g, k:k + 8, :]
                    some = v if some is None else some + v
                total = total + (some if a == 0 else pltpu.roll(some, 2 * a, 0))
            out.append(total)
        return out

    lane = lax.broadcasted_iota(jnp.int32, (128, 128), 1)

    def half_rows(q, g):
        return pl.ds(pl.multiple_of(q * B + g * 128, 128), 128)

    def to_lanes(g, at):
        row_sib[g, at:at + 8, :] = jnp.transpose(mat[...])[0:8, :]

    def to_rows(v, g, out):
        wide = jnp.transpose(jnp.concatenate([v, jnp.zeros((120, 128), f32)], axis=0))
        for q in range(8):
            out[q * B + g * 128:q * B + (g + 1) * 128, :] = jnp.broadcast_to(wide[:, q:q + 1], (128, 128))

    def row_first(col, acc):
        def body(q, _):
            rows = pl.ds(pl.multiple_of(q * B, B), B)
            total = t_exp[rows, tile(0, 0)] * col[0:1, :]
            for s in range(1, NZ):
                total = total + t_exp[rows, tile(s, 0)] * col[s:s + 1, :]
            acc[rows, :] = total
            return 0

        lax.fori_loop(0, 8, body, 0)

    def row_last(col, acc, g):
        mat[...] = jnp.zeros((128, 128), f32)

        def body(q, _):
            rows = half_rows(q, g)
            total = acc[rows, :]
            for s in range(NZ):
                total = total + t_exp[rows, tile(s, 1)] * col[s:s + 1, :]
            mat[...] = jnp.where(lane == q, jnp.sum(total, axis=1, keepdims=True), mat[...])
            return 0

        lax.fori_loop(0, 8, body, 0)

    def partition_sum(g):
        mat[...] = jnp.zeros((128, 128), f32)

        def body(q, _):
            total = jnp.sum(part[half_rows(q, g), :], axis=1, keepdims=True)
            mat[...] = jnp.where(lane == q, total, mat[...])
            return 0

        lax.fori_loop(0, 8, body, 0)

    def col_part(g, start, tiles):
        def body(q, acc):
            rows = half_rows(q, g)
            scale = row_b[rows, :]
            return tuple(
                v + jnp.sum((t_exp[rows, at] * scale).reshape(16, 8, 128), axis=0) for v, at in zip(acc, tiles)
            )

        return lax.fori_loop(0, 8, body, start)

    def row_to_col(n):
        zeros = jnp.zeros((8, 128), f32)
        both = [tile(s, h) for h in (0, 1) for s in range(NZ)]
        first = finish_row(n, 0)
        to_rows(1.0 / (CROPS * first[0]), 0, row_b)
        acc = col_part(0, (zeros,) * 16, both)
        second = finish_row(n, 1)
        to_rows(1.0 / (CROPS * second[0]), 1, row_b)
        for h in (0, 1):
            for s, v in enumerate(col_part(1, acc[h * 8:h * 8 + 8], both[h * 8:h * 8 + 8])):
                col_send[n + 1, h, s:s + 1, :] = jnp.sum(v, axis=0, keepdims=True)
            start_col(n + 1, h)
        return first[1:] + second[1:]

    def col_to_row(n, acc):
        first = finish_col(n, 0)
        row_first(first, acc)
        second = finish_col(n, 1)
        for g in (0, 1):
            row_last(second, acc, g)
            to_lanes(g, OFFSET[n])
            start_sibling(n, g)
        for g in (0, 1):
            start_row(n, g)
        return first, second

    start_col(0, 0)
    start_col(0, 1)
    crop_last(1)
    crop_wait(1)
    for s in range(4):
        student_slot(s)
    col_to_row(0, row_a)
    for s in range(4, 8):
        student_slot(s)
    row_to_col(0)
    for g in (0, 1):
        partition_sum(g)
        to_lanes(g, OFFSET[1] + 8)
    for q in range(8):
        stud_t[:, q * B:(q + 1) * B] = jnp.transpose(stud[q * B:(q + 1) * B, :].astype(f32)).astype(bf16)
    col_to_row(1, row_a)
    partition = row_to_col(1)
    for g in (0, 1):
        to_rows((loss_scale / student_temp) / partition[g], g, row_a)

    def scale_student(i, _):
        rows = pl.ds(pl.multiple_of(i * 64, 64), 64)
        scale = row_a[rows, :]
        for s in range(NZ):
            for h in (0, 1):
                s_exp[rows, tile(s, h)] = s_exp[rows, tile(s, h)] * scale
        return 0

    lax.fori_loop(0, ROWS // 64, scale_student, 0)
    col = col_to_row(2, part)

    def scale_teacher(i, _):
        rows = pl.ds(pl.multiple_of(i * 64, 64), 64)
        for s in range(NZ):
            for h in (0, 1):
                t_exp[rows, tile(s, h)] = t_exp[rows, tile(s, h)] * col[h][s:s + 1, :]
        return 0

    lax.fori_loop(0, ROWS // 64, scale_teacher, 0)
    for g in (0, 1):
        (row_total,) = finish_row(2, g)
        to_rows((loss_scale / student_temp) / row_total, g, row_b)

    def grad_part(start, height, slots):
        for r in range(start, start + height, 16):
            rows = slice(r, r + 16)
            scale = row_b[rows, :]
            for s in slots:
                for h in (0, 1):
                    at = tile(s, h)
                    grad[rows, at] = (s_exp[rows, at] - t_exp[rows, at] * scale).astype(bf16)

    def chunk_dot(s):
        chunk[s] = jnp.dot(stud_t[...], grad[:, s * B:(s + 1) * B], preferred_element_type=f32)

    def ring(m, d):
        s = 4 - m if d == 0 else 4 + m
        _, to1, to2, first, then = ways[d]
        for p in first if m == 0 else first + then:
            rows = slice(p * PIECE, (p + 1) * PIECE)
            at = pl.ds(p * PIECE, PIECE)
            value = chunk[s, rows, :]
            if m >= 2:
                wait_recv(ring_recv.at[2 * (m - 1) + d, at], rg_rs.at[m - 1, d, p])
                value = value + ring_recv[2 * (m - 1) + d, rows, :].astype(f32)
            if m == 2 and p in first:
                wait_recv(ring_recv.at[d, at], rg_rs.at[0, d, p])
                value = value + ring_recv[d, rows, :].astype(f32)
            ring_send[2 * m + d, rows, :] = value.astype(bf16)
            copy(
                ring_send.at[2 * m + d, at], ring_recv.at[2 * m + d, at], RING, rg_rs.at[m, d, p],
                to2 if m == 0 else to1,
            ).start()

    def u_dot(q):
        return jnp.dot(grad[q * B:(q + 1) * B, :], protos[...], preferred_element_type=f32)

    us = {}

    def u_pair(j, slots):
        grad_part((2 * j + 1) * B, B, slots)
        grad_part(2 * j * B, B, slots)
        u_send[j] = u_dot(2 * j + 1).astype(bf16)
        cp = copy(u_send.at[j], u_sib.at[j], US, us_rs.at[j], sibling)
        cp.start()
        us[j] = cp
        u_ref[j] = u_dot(2 * j)

    Q = B // NX
    mine = pl.ds(pl.multiple_of(x * Q, Q), Q)

    def v_start(j):
        us[j].wait_recv()
        total = u_ref[j] + u_sib[j].astype(f32)
        if j == 0:
            u_ref[j] = total
        v_send[j] = total.astype(bf16)
        for b in (2, 1, 3, 0):
            if (j, b) == (0, 0):
                continue
            t = ((NY - j) % NY) * NX + (NX - b) % NX - 1
            at = pl.multiple_of(((x + b) % NX) * Q, Q)
            copy(v_send.at[j, pl.ds(at, Q)], v_recv.at[t], V, vq_rs.at[0], dev(0, j, 0, b)).start()

    grad_part(0, ROWS, (3,))
    chunk_dot(3)
    ring(1, 0)
    grad_part(0, ROWS, (5,))
    chunk_dot(5)
    ring(1, 1)
    grad_part(0, ROWS, (4,))
    chunk_dot(4)
    ring(0, 0)
    ring(0, 1)
    rest = (0, 1, 2, 6, 7)
    u_pair(2, rest)
    u_pair(1, rest)
    v_start(2)
    u_pair(3, rest)
    v_start(1)
    u_pair(0, rest)
    chunk_dot(2)
    chunk_dot(6)
    ring(2, 0)
    ring(2, 1)
    v_start(3)
    v_start(0)
    chunk_dot(1)
    chunk_dot(7)
    chunk_dot(0)
    ring(3, 0)
    ring(3, 1)

    wait_recv(v_recv, vq_rs.at[0])
    total = u_ref[0, mine, :]
    for i in range(N_YX):
        total = total + v_recv[i].astype(f32)
    unit, inverse = unit_rows(student_ref[mine, :])
    q_full[mine, :] = (inverse * (total - unit * jnp.sum(unit * total, axis=1, keepdims=True))).astype(bf16)
    for b in (2, 1, 3):
        copy(q_full.at[mine], q_full.at[mine], QS, vq_rs.at[1], dev(0, 0, 0, b)).start()

    total = chunk[0]
    for d in (0, 1):
        for p in every:
            wait_recv(ring_recv.at[6 + d, pl.ds(p * PIECE, PIECE)], rg_rs.at[3, d, p])
        total = total + ring_recv[6 + d].astype(f32)
    total = jnp.transpose(total)
    unit, inverse = unit_rows(proto_ref[...])
    gp_ref[...] = inverse * (total - unit * jnp.sum(unit * total, axis=1, keepdims=True))

    wait_recv(q_full.at[pl.ds(0, (NX - 1) * Q)], vq_rs.at[1])
    gs_ref[...] = q_full[...].astype(f32)

    wait_send(protos.at[pl.ds(0, 7 * B)], AG)
    for w in (0, 1):
        wait_send(crops[w].at[pl.ds(0, 3 * B)], CROP + w)
        wait_send(crops[w].at[pl.ds(0, 4 * B)], FORWARD + w)
    wait_send(col_recv, COL)
    wait_send(row_sib, SIB)
    wait_send(row_recv, ROW)
    wait_send(ring_recv.at[pl.ds(0, 7)], RING)
    wait_send(u_sib, US)
    wait_send(v_recv, V)
    wait_send(q_full.at[pl.ds(0, (NX - 1) * Q)], QS)


def shards(student_feat, teacher_feat, prototypes):
    vmem = pltpu.VMEM
    dma = pltpu.SemaphoreType.DMA
    sems = [
        dma((GROUPS,)), dma((3, 2, SUB)), dma((2,)), dma((2, 2, 2)), dma((2, 2)), dma((2,)), dma((SWEEPS, 2)), dma((SWEEPS, 2)),
        dma((SWEEPS, 2)), dma((4, 2, SUB)), dma((NY,)), dma((2,)),
    ]
    return pl.pallas_call(
        kernel,
        out_shape=[jax.ShapeDtypeStruct((B, B), f32), jax.ShapeDtypeStruct((B, B), f32)],
        in_specs=[pl.BlockSpec(memory_space=pltpu.VMEM)] * 3,
        out_specs=[pl.BlockSpec(memory_space=pltpu.VMEM)] * 2,
        scratch_shapes=[
            vmem((COLS, B), bf16),
            vmem((ROWS, B), bf16),
            vmem((ROWS, B), bf16),
            vmem((B, ROWS), bf16),
            vmem((ROWS, COLS), f32),
            vmem((ROWS, COLS), f32),
            vmem((ROWS, COLS), bf16),
            vmem((ROWS, 128), f32),
            vmem((ROWS, 128), f32),
            vmem((ROWS, 128), f32),
            vmem((128, 128), f32),
            vmem((SWEEPS, 2, 8, 128), f32),
            vmem((SWEEPS, 2, NZ - 1, 8, 128), f32),
            vmem((2, OFFSET[-1], 128), f32),
            vmem((2, OFFSET[-1], 128), f32),
            vmem((2, OFFSET[-1], 128), f32),
            vmem((2, N_YX * OFFSET[-1], 128), f32),
            vmem((NZ, B, B), f32),
            vmem((8, B, B), bf16),
            vmem((8, B, B), bf16),
            vmem((NY, B, B), f32),
            vmem((NY, B, B), bf16),
            vmem((NY, B, B), bf16),
            vmem((NY, B, B), bf16),
            vmem((N_YX, B // NX, B), bf16),
            vmem((B, B), bf16),
        ] + sems,
        compiler_params=pltpu.CompilerParams(
            collective_id=0, has_side_effects=True, vmem_limit_bytes=63 * 2**20
        ),
    )(student_feat, teacher_feat, prototypes)


def solution(mesh):
    in_specs = (P("dp", None), P("dp", None), P(("dp", "proto"), None))
    out_specs = (P("dp", None), P(("dp", "proto"), None))
    return jax.shard_map(shards, mesh=mesh, in_specs=in_specs, out_specs=out_specs, check_vma=False)
```

```python
import math

import jax
import jax.numpy as jnp
from jax import lax
from jax.experimental import pallas as pl
from jax.experimental.pallas import tpu as pltpu
from jax.sharding import PartitionSpec as P

NZ, NY, NX, NC = 8, 4, 4, 2
B = 256
ROWS = NY * NC * B
COLS = NZ * B
CROPS = 16384
PROTOS = 65536
SWEEPS = 3
teacher_temp = 0.07
student_temp = 0.1
loss_scale = 1024.0
epsilon = 1e-06
LOG2E = math.log2(math.e)
MESH = pl.DeviceIdType.MESH
NT = (((1,), (1,)), ((), ()))
f32 = jnp.float32
bf16 = jnp.bfloat16
SUB = 4
PIECE = B // SUB
H = B // 2
N_YX = NY * NX - 1
OFFSET = (0, 8, 24, 32)
AG, CROP, FORWARD, COL, SIB, ROW, RING, US, V, QS, GROUPS = 0, 1, 3, 5, 6, 7, 8, 9, 10, 11, 12


def unit_rows(matrix):
    values = matrix.astype(f32)
    inverse = lax.rsqrt(jnp.sum(values * values, axis=-1, keepdims=True) + epsilon)
    return values * inverse, inverse


def kernel(
    student_ref, teacher_ref, proto_ref, gs_ref, gp_ref,
    protos, teach, stud, stud_t, t_exp, s_exp, grad, part, row_a, row_b, mat,
    col_send, col_recv, row_sib, row_send, sib_recv, row_recv,
    chunk, ring_send, ring_recv, u_ref, u_send, u_sib, v_send, v_recv, q_full,
    ss, ag_rs, far_ag_rs, hop_rs, far_rs, fw_rs, col_rs, sib_rs, row_rs, rg_rs, us_rs, vq_rs,
):
    dp = lax.axis_index("dp")
    x = lax.axis_index("proto")
    z, y, c = dp // (NY * NC), (dp // NC) % NY, dp % NC

    def dev(dz, dy, flip, dx):
        core = 1 - c if flip else c
        return ((((z + dz) % NZ) * NY + (y + dy) % NY) * NC + core, (x + dx) % NX)

    right, left, sibling = dev(1, 0, 0, 0), dev(NZ - 1, 0, 0, 0), dev(0, 0, 1, 0)
    right2, left2 = dev(2, 0, 0, 0), dev(NZ - 2, 0, 0, 0)
    up, down = dev(0, 1, 0, 0), dev(0, NY - 1, 0, 0)
    z_peers = [(o, dev(o, 0, 0, 0)) for o in (4, 3, 5, 2, 6, 1, 7)]
    far = sorted(
        ((a, b) for a in range(NY) for b in range(NX) if (a, b) != (0, 0)),
        key=lambda ab: -min(ab[0], NY - ab[0]) - min(ab[1], NX - ab[1]),
    )
    yx_peers = [((a, b), dev(0, a, 0, b)) for a, b in far]

    def copy(src, dst, group, rs, to):
        return pltpu.make_async_remote_copy(
            src_ref=src, dst_ref=dst, send_sem=ss.at[group], recv_sem=rs, device_id=to, device_id_type=MESH
        )

    def wait_recv(ref, rs):
        copy(ref, ref, 0, rs, right).wait_recv()

    def wait_send(ref, group):
        copy(ref, ref, group, vq_rs.at[0], right).wait_send()

    barrier = pltpu.get_barrier_semaphore()
    near = [right2, left2, right, left, up, down, sibling] + [dev(0, 0, 0, b) for b in (2, 1, 3)]
    for peer in near:
        pl.semaphore_signal(barrier, inc=1, device_id=peer, device_id_type=MESH)

    protos[0:B, :] = unit_rows(proto_ref[...])[0].astype(bf16)
    teach[0:B, :] = unit_rows(teacher_ref[...])[0].astype(bf16)
    stud[0:B, :] = unit_rows(student_ref[...])[0].astype(bf16)
    pl.semaphore_wait(barrier, len(near))

    low, high = tuple(range(SUB // 2)), tuple(range(SUB // 2, SUB))
    every = low + high
    ways = ((0, right, right2, low, high), (1, left, left2, high, low))

    def block(k, d, p):
        slot = (NZ - k) % NZ if d == 0 else k
        return protos.at[pl.ds(slot * B + p * PIECE, PIECE)]

    def ag_step(k):
        for i in range(SUB):
            for d, to1, to2, first, then in ways:
                p = (first + then)[i]
                if k > 0:
                    wait_recv(block(k, d, p), ag_rs.at[k - 1, d, p])
                if k == 2 and p in first:
                    copy(block(2, d, p), block(4, d, p), AG, far_ag_rs.at[d], to2).start()
                copy(block(k, d, p), block(k + 1, d, p), AG, ag_rs.at[k, d, p], to1).start()

    def ag_wait():
        for d in (0, 1):
            for p in every:
                wait_recv(block(3, d, p), ag_rs.at[2, d, p])

    def ag_wait_far():
        for d in (0, 1):
            wait_recv(protos.at[pl.ds(0, H)], far_ag_rs.at[d])

    hop, last = {}, {}
    crops = (teach, stud)

    def forward(w, j):
        ref = crops[w]
        copy(
            ref.at[pl.ds(2 * j * B, B)], ref.at[pl.ds((2 * j + 1) * B, B)], FORWARD + w, fw_rs.at[w], sibling
        ).start()

    def crop_start(w):
        ref = crops[w]
        for first in (0, 1):
            for d, to, j in ((0, up, 3), (1, down, 1)):
                h = first if d == 0 else 1 - first
                cp = copy(
                    ref.at[pl.ds(h * H, H)], ref.at[pl.ds(2 * j * B + h * H, H)],
                    CROP + w, hop_rs.at[w, d, h], to,
                )
                cp.start()
                hop[(w, d, h)] = cp
        forward(w, 0)

    def crop_relay(w):
        ref = crops[w]
        for d, to, j in ((0, up, 3), (1, down, 1)):
            hop[(w, d, d)].wait_recv()
            cp = copy(
                ref.at[pl.ds(2 * j * B + d * H, H)], ref.at[pl.ds(4 * B + d * H, H)],
                CROP + w, far_rs.at[w, d], to,
            )
            cp.start()
            last[(w, d)] = cp
        for d, j in ((0, 3), (1, 1)):
            hop[(w, d, 1 - d)].wait_recv()
            forward(w, j)

    def crop_last(w):
        for d in (0, 1):
            last[(w, d)].wait_recv()
        forward(w, 2)

    def crop_wait(w):
        wait_recv(crops[w].at[pl.ds(0, NY * B)], fw_rs.at[w])

    def teacher_slot(s):
        cols = slice(s * B, (s + 1) * B)
        dots = lax.dot_general(teach[...], protos[cols, :], NT, preferred_element_type=f32)
        values = jnp.exp2(dots * (LOG2E / teacher_temp))
        t_exp[:, cols] = values
        total = jnp.sum(values, axis=0, keepdims=True)
        for h in (0, 1):
            col_send[0, h, s:s + 1, :] = total[:, h * 128:(h + 1) * 128]

    def student_slot(s):
        cols = slice(s * B, (s + 1) * B)
        dots = lax.dot_general(stud[...], protos[cols, :], NT, preferred_element_type=f32)
        values = jnp.exp2(dots * (LOG2E / student_temp))
        s_exp[:, cols] = values
        both = values[:, :128] + values[:, 128:]
        part[...] = both if s == 0 else part[...] + both

    ag_step(0)
    crop_start(0)
    crop_start(1)
    ag_step(1)
    crop_relay(0)
    ag_step(2)
    crop_last(0)
    crop_wait(0)
    for s in (0, 1, 7, 2, 6):
        teacher_slot(s)
    crop_relay(1)
    ag_wait()
    teacher_slot(3)
    teacher_slot(5)
    ag_wait_far()
    teacher_slot(4)

    def tile(s, h):
        return slice(s * B + h * 128, s * B + (h + 1) * 128)

    def start_col(n, h):
        for o, peer in z_peers:
            copy(col_send.at[n, h], col_recv.at[n, h, NZ - o - 1], COL, col_rs.at[n, h], peer).start()

    def finish_col(n, h):
        total = col_send[n, h]
        wait_recv(col_recv.at[n, h], col_rs.at[n, h])
        for o in range(1, NZ):
            total = total + pltpu.roll(col_recv[n, h, o - 1], o, 0)
        return 1.0 / (PROTOS * total)

    def start_sibling(n, g):
        at = pl.ds(OFFSET[n], OFFSET[n + 1] - OFFSET[n])
        copy(row_sib.at[g, at], sib_recv.at[g, at], SIB, sib_rs.at[n, g], sibling).start()

    even = lax.broadcasted_iota(jnp.int32, (8, 128), 0) % 2 == 0

    def swap(v):
        return jnp.where(even, pltpu.roll(v, 7, 0), pltpu.roll(v, 1, 0))

    def start_row(n, g):
        start, height = OFFSET[n], OFFSET[n + 1] - OFFSET[n]
        at = pl.ds(start, height)
        wait_recv(sib_recv.at[g, at], sib_rs.at[n, g])
        for i in range(start, start + height, 8):
            row_send[g, i:i + 8, :] = row_sib[g, i:i + 8, :] + swap(sib_recv[g, i:i + 8, :])
        for (a, b), peer in yx_peers:
            t = ((NY - a) % NY) * NX + (NX - b) % NX - 1
            to = row_recv.at[g, pl.ds(N_YX * start + t * height, height)]
            copy(row_send.at[g, at], to, ROW, row_rs.at[n, g], peer).start()

    def finish_row(n, g):
        start, height = OFFSET[n], OFFSET[n + 1] - OFFSET[n]
        wait_recv(row_recv.at[g, pl.ds(N_YX * start, N_YX * height)], row_rs.at[n, g])
        out = []
        for i in range(0, height, 8):
            total = row_send[g, start + i:start + i + 8, :]
            for a in range(NY):
                some = None
                for b in range(NX):
                    if (a, b) == (0, 0):
                        continue
                    k = N_YX * start + (a * NX + b - 1) * height + i
                    v = row_recv[g, k:k + 8, :]
                    some = v if some is None else some + v
                total = total + (some if a == 0 else pltpu.roll(some, 2 * a, 0))
            out.append(total)
        return out

    lane = lax.broadcasted_iota(jnp.int32, (128, 128), 1)

    def half_rows(q, g):
        return pl.ds(pl.multiple_of(q * B + g * 128, 128), 128)

    def to_lanes(g, at):
        row_sib[g, at:at + 8, :] = jnp.transpose(mat[...])[0:8, :]

    def to_rows(v, g, out):
        wide = jnp.transpose(jnp.concatenate([v, jnp.zeros((120, 128), f32)], axis=0))
        for q in range(8):
            out[q * B + g * 128:q * B + (g + 1) * 128, :] = jnp.broadcast_to(wide[:, q:q + 1], (128, 128))

    def row_first(col, acc):
        def body(q, _):
            rows = pl.ds(pl.multiple_of(q * B, B), B)
            total = t_exp[rows, tile(0, 0)] * col[0:1, :]
            for s in range(1, NZ):
                total = total + t_exp[rows, tile(s, 0)] * col[s:s + 1, :]
            acc[rows, :] = total
            return 0

        lax.fori_loop(0, 8, body, 0)

    def row_last(col, acc, g):
        wide = jnp.zeros((128, 128), f32)
        for q in range(8):
            rows = slice(q * B + g * 128, q * B + (g + 1) * 128)
            total = acc[rows, :]
            for s in range(NZ):
                total = total + t_exp[rows, tile(s, 1)] * col[s:s + 1, :]
            wide = jnp.where(lane == q, jnp.sum(total, axis=1, keepdims=True), wide)
        mat[...] = wide

    def partition_sum(g):
        mat[...] = jnp.zeros((128, 128), f32)

        def body(q, _):
            total = jnp.sum(part[half_rows(q, g), :], axis=1, keepdims=True)
            mat[...] = jnp.where(lane == q, total, mat[...])
            return 0

        lax.fori_loop(0, 8, body, 0)

    def col_part(g, acc, tiles):
        for q in range(8):
            rows = slice(q * B + g * 128, q * B + (g + 1) * 128)
            scale = row_b[rows, :]
            acc = tuple(
                v + jnp.sum((t_exp[rows, at] * scale).reshape(16, 8, 128), axis=0) for v, at in zip(acc, tiles)
            )
        return acc

    def row_to_col(n):
        zeros = jnp.zeros((8, 128), f32)
        both = [tile(s, h) for h in (0, 1) for s in range(NZ)]
        first = finish_row(n, 0)
        to_rows(1.0 / (CROPS * first[0]), 0, row_b)
        acc = col_part(0, (zeros,) * 16, both)
        second = finish_row(n, 1)
        to_rows(1.0 / (CROPS * second[0]), 1, row_b)
        for h in (0, 1):
            for s, v in enumerate(col_part(1, acc[h * 8:h * 8 + 8], both[h * 8:h * 8 + 8])):
                col_send[n + 1, h, s:s + 1, :] = jnp.sum(v, axis=0, keepdims=True)
            start_col(n + 1, h)
        return first[1:] + second[1:]

    def col_to_row(n, acc):
        first = finish_col(n, 0)
        row_first(first, acc)
        second = finish_col(n, 1)
        for g in (0, 1):
            row_last(second, acc, g)
            to_lanes(g, OFFSET[n])
            start_sibling(n, g)
        for g in (0, 1):
            start_row(n, g)
        return first, second

    start_col(0, 0)
    start_col(0, 1)
    crop_last(1)
    crop_wait(1)
    for s in range(4):
        student_slot(s)
    col_to_row(0, row_a)
    for s in range(4, 8):
        student_slot(s)
    row_to_col(0)
    for g in (0, 1):
        partition_sum(g)
        to_lanes(g, OFFSET[1] + 8)
    for q in range(8):
        stud_t[:, q * B:(q + 1) * B] = jnp.transpose(stud[q * B:(q + 1) * B, :].astype(f32)).astype(bf16)
    col_to_row(1, row_a)
    partition = row_to_col(1)
    for g in (0, 1):
        to_rows((loss_scale / student_temp) / partition[g], g, row_a)

    def scale_student(i, _):
        rows = pl.ds(pl.multiple_of(i * 64, 64), 64)
        scale = row_a[rows, :]
        for s in range(NZ):
            for h in (0, 1):
                s_exp[rows, tile(s, h)] = s_exp[rows, tile(s, h)] * scale
        return 0

    lax.fori_loop(0, ROWS // 64, scale_student, 0)
    col = col_to_row(2, part)

    def scale_teacher(i, _):
        rows = pl.ds(pl.multiple_of(i * 64, 64), 64)
        for s in range(NZ):
            for h in (0, 1):
                t_exp[rows, tile(s, h)] = t_exp[rows, tile(s, h)] * col[h][s:s + 1, :]
        return 0

    lax.fori_loop(0, ROWS // 64, scale_teacher, 0)
    for g in (0, 1):
        (row_total,) = finish_row(2, g)
        to_rows((loss_scale / student_temp) / row_total, g, row_b)

    def grad_part(start, height, slots):
        for r in range(start, start + height, 16):
            rows = slice(r, r + 16)
            scale = row_b[rows, :]
            for s in slots:
                for h in (0, 1):
                    at = tile(s, h)
                    grad[rows, at] = (s_exp[rows, at] - t_exp[rows, at] * scale).astype(bf16)

    def chunk_dot(s):
        chunk[s] = jnp.dot(stud_t[...], grad[:, s * B:(s + 1) * B], preferred_element_type=f32)

    def ring(m, d):
        s = 4 - m if d == 0 else 4 + m
        _, to1, to2, first, then = ways[d]
        for p in first if m == 0 else first + then:
            rows = slice(p * PIECE, (p + 1) * PIECE)
            at = pl.ds(p * PIECE, PIECE)
            value = chunk[s, rows, :]
            if m >= 2:
                wait_recv(ring_recv.at[2 * (m - 1) + d, at], rg_rs.at[m - 1, d, p])
                value = value + ring_recv[2 * (m - 1) + d, rows, :].astype(f32)
            if m == 2 and p in first:
                wait_recv(ring_recv.at[d, at], rg_rs.at[0, d, p])
                value = value + ring_recv[d, rows, :].astype(f32)
            ring_send[2 * m + d, rows, :] = value.astype(bf16)
            copy(
                ring_send.at[2 * m + d, at], ring_recv.at[2 * m + d, at], RING, rg_rs.at[m, d, p],
                to2 if m == 0 else to1,
            ).start()

    def u_dot(q):
        return jnp.dot(grad[q * B:(q + 1) * B, :], protos[...], preferred_element_type=f32)

    us = {}

    def u_grad(j, slots):
        grad_part((2 * j + 1) * B, B, slots)
        grad_part(2 * j * B, B, slots)

    def u_pair(j):
        u_send[j] = u_dot(2 * j + 1).astype(bf16)
        u_ref[j] = u_dot(2 * j)

    def u_start(j):
        cp = copy(u_send.at[j], u_sib.at[j], US, us_rs.at[j], sibling)
        cp.start()
        us[j] = cp

    Q = B // NX
    mine = pl.ds(pl.multiple_of(x * Q, Q), Q)

    def v_start(j):
        us[j].wait_recv()
        total = u_ref[j] + u_sib[j].astype(f32)
        if j == 0:
            u_ref[j] = total
        v_send[j] = total.astype(bf16)
        for b in (2, 1, 3, 0):
            if (j, b) == (0, 0):
                continue
            t = ((NY - j) % NY) * NX + (NX - b) % NX - 1
            at = pl.multiple_of(((x + b) % NX) * Q, Q)
            copy(v_send.at[j, pl.ds(at, Q)], v_recv.at[t], V, vq_rs.at[0], dev(0, j, 0, b)).start()

    rest = (0, 1, 2, 6, 7)
    grad_part(0, ROWS, (3,))
    chunk_dot(3)
    grad_part(0, ROWS, (5,))
    ring(1, 0)
    chunk_dot(5)
    grad_part(0, ROWS, (4,))
    ring(1, 1)
    chunk_dot(4)
    u_grad(2, rest)
    ring(0, 0)
    ring(0, 1)
    u_pair(2)
    u_grad(1, rest)
    u_start(2)
    u_pair(1)
    u_grad(3, rest)
    u_start(1)
    v_start(2)
    u_pair(3)
    u_grad(0, rest)
    u_start(3)
    v_start(1)
    u_pair(0)
    u_start(0)
    v_start(3)
    chunk_dot(2)
    chunk_dot(6)
    chunk_dot(1)
    v_start(0)
    ring(2, 0)
    ring(2, 1)
    chunk_dot(7)
    chunk_dot(0)
    ring(3, 0)
    ring(3, 1)

    wait_recv(v_recv, vq_rs.at[0])
    total = u_ref[0, mine, :]
    for i in range(N_YX):
        total = total + v_recv[i].astype(f32)
    unit, inverse = unit_rows(student_ref[mine, :])
    q_full[mine, :] = (inverse * (total - unit * jnp.sum(unit * total, axis=1, keepdims=True))).astype(bf16)
    for b in (2, 1, 3):
        copy(q_full.at[mine], q_full.at[mine], QS, vq_rs.at[1], dev(0, 0, 0, b)).start()

    total = chunk[0]
    for d in (0, 1):
        for p in every:
            wait_recv(ring_recv.at[6 + d, pl.ds(p * PIECE, PIECE)], rg_rs.at[3, d, p])
        total = total + ring_recv[6 + d].astype(f32)
    total = jnp.transpose(total)
    unit, inverse = unit_rows(proto_ref[...])
    gp_ref[...] = inverse * (total - unit * jnp.sum(unit * total, axis=1, keepdims=True))

    wait_recv(q_full.at[pl.ds(0, (NX - 1) * Q)], vq_rs.at[1])
    gs_ref[...] = q_full[...].astype(f32)

    wait_send(protos.at[pl.ds(0, 7 * B)], AG)
    for w in (0, 1):
        wait_send(crops[w].at[pl.ds(0, 3 * B)], CROP + w)
        wait_send(crops[w].at[pl.ds(0, 4 * B)], FORWARD + w)
    wait_send(col_recv, COL)
    wait_send(row_sib, SIB)
    wait_send(row_recv, ROW)
    wait_send(ring_recv.at[pl.ds(0, 7)], RING)
    wait_send(u_sib, US)
    wait_send(v_recv, V)
    wait_send(q_full.at[pl.ds(0, (NX - 1) * Q)], QS)


def shards(student_feat, teacher_feat, prototypes):
    vmem = pltpu.VMEM
    dma = pltpu.SemaphoreType.DMA
    sems = [
        dma((GROUPS,)), dma((3, 2, SUB)), dma((2,)), dma((2, 2, 2)), dma((2, 2)), dma((2,)), dma((SWEEPS, 2)), dma((SWEEPS, 2)),
        dma((SWEEPS, 2)), dma((4, 2, SUB)), dma((NY,)), dma((2,)),
    ]
    return pl.pallas_call(
        kernel,
        out_shape=[jax.ShapeDtypeStruct((B, B), f32), jax.ShapeDtypeStruct((B, B), f32)],
        in_specs=[pl.BlockSpec(memory_space=pltpu.VMEM)] * 3,
        out_specs=[pl.BlockSpec(memory_space=pltpu.VMEM)] * 2,
        scratch_shapes=[
            vmem((COLS, B), bf16),
            vmem((ROWS, B), bf16),
            vmem((ROWS, B), bf16),
            vmem((B, ROWS), bf16),
            vmem((ROWS, COLS), f32),
            vmem((ROWS, COLS), f32),
            vmem((ROWS, COLS), bf16),
            vmem((ROWS, 128), f32),
            vmem((ROWS, 128), f32),
            vmem((ROWS, 128), f32),
            vmem((128, 128), f32),
            vmem((SWEEPS, 2, 8, 128), f32),
            vmem((SWEEPS, 2, NZ - 1, 8, 128), f32),
            vmem((2, OFFSET[-1], 128), f32),
            vmem((2, OFFSET[-1], 128), f32),
            vmem((2, OFFSET[-1], 128), f32),
            vmem((2, N_YX * OFFSET[-1], 128), f32),
            vmem((NZ, B, B), f32),
            vmem((8, B, B), bf16),
            vmem((8, B, B), bf16),
            vmem((NY, B, B), f32),
            vmem((NY, B, B), bf16),
            vmem((NY, B, B), bf16),
            vmem((NY, B, B), bf16),
            vmem((N_YX, B // NX, B), bf16),
            vmem((B, B), bf16),
        ] + sems,
        compiler_params=pltpu.CompilerParams(
            collective_id=0, has_side_effects=True, vmem_limit_bytes=63 * 2**20
        ),
    )(student_feat, teacher_feat, prototypes)


def solution(mesh):
    in_specs = (P("dp", None), P("dp", None), P(("dp", "proto"), None))
    out_specs = (P("dp", None), P(("dp", "proto"), None))
    return jax.shard_map(shards, mesh=mesh, in_specs=in_specs, out_specs=out_specs, check_vma=False)
```

```python
import math

import jax
import jax.numpy as jnp
from jax import lax
from jax.experimental import pallas as pl
from jax.experimental.pallas import tpu as pltpu
from jax.sharding import PartitionSpec as P

NZ, NY, NX, NC = 8, 4, 4, 2
B = 256
ROWS = NY * NC * B
COLS = NZ * B
CROPS = 16384
PROTOS = 65536
SWEEPS = 3
teacher_temp = 0.07
student_temp = 0.1
loss_scale = 1024.0
epsilon = 1e-06
LOG2E = math.log2(math.e)
MESH = pl.DeviceIdType.MESH
NT = (((1,), (1,)), ((), ()))
f32 = jnp.float32
bf16 = jnp.bfloat16
SUB = 4
PIECE = B // SUB
H = B // 2
N_YX = NY * NX - 1
OFFSET = (0, 8, 24, 32)
AG, CROP, FORWARD, COL, SIB, ROW, RING, US, V, QS, GROUPS = 0, 1, 3, 5, 6, 7, 8, 9, 10, 11, 12


def unit_rows(matrix):
    values = matrix.astype(f32)
    inverse = lax.rsqrt(jnp.sum(values * values, axis=-1, keepdims=True) + epsilon)
    return values * inverse, inverse


def kernel(
    student_ref, teacher_ref, proto_ref, gs_ref, gp_ref,
    protos, teach, stud, stud_t, t_exp, s_exp, grad, part, row_a, row_b, mat,
    col_send, col_recv, row_sib, row_send, sib_recv, row_recv,
    chunk, ring_send, ring_recv, u_ref, u_send, u_sib, v_send, v_recv, q_full,
    ss, ag_rs, far_ag_rs, hop_rs, far_rs, fw_rs, col_rs, sib_rs, row_rs, rg_rs, us_rs, vq_rs,
):
    dp = lax.axis_index("dp")
    x = lax.axis_index("proto")
    z, y, c = dp // (NY * NC), (dp // NC) % NY, dp % NC

    def dev(dz, dy, flip, dx):
        core = 1 - c if flip else c
        return ((((z + dz) % NZ) * NY + (y + dy) % NY) * NC + core, (x + dx) % NX)

    right, left, sibling = dev(1, 0, 0, 0), dev(NZ - 1, 0, 0, 0), dev(0, 0, 1, 0)
    right2, left2 = dev(2, 0, 0, 0), dev(NZ - 2, 0, 0, 0)
    up, down = dev(0, 1, 0, 0), dev(0, NY - 1, 0, 0)
    z_peers = [(o, dev(o, 0, 0, 0)) for o in (4, 3, 5, 2, 6, 1, 7)]
    far = sorted(
        ((a, b) for a in range(NY) for b in range(NX) if (a, b) != (0, 0)),
        key=lambda ab: -min(ab[0], NY - ab[0]) - min(ab[1], NX - ab[1]),
    )
    yx_peers = [((a, b), dev(0, a, 0, b)) for a, b in far]

    def copy(src, dst, group, rs, to):
        return pltpu.make_async_remote_copy(
            src_ref=src, dst_ref=dst, send_sem=ss.at[group], recv_sem=rs, device_id=to, device_id_type=MESH
        )

    def wait_recv(ref, rs):
        copy(ref, ref, 0, rs, right).wait_recv()

    def wait_send(ref, group):
        copy(ref, ref, group, vq_rs.at[0], right).wait_send()

    barrier = pltpu.get_barrier_semaphore()
    near = [right2, left2, right, left, up, down, sibling] + [dev(0, 0, 0, b) for b in (2, 1, 3)]
    for peer in near:
        pl.semaphore_signal(barrier, inc=1, device_id=peer, device_id_type=MESH)

    protos[0:B, :] = unit_rows(proto_ref[...])[0].astype(bf16)
    teach[0:B, :] = unit_rows(teacher_ref[...])[0].astype(bf16)
    stud[0:B, :] = unit_rows(student_ref[...])[0].astype(bf16)
    pl.semaphore_wait(barrier, len(near))

    low, high = tuple(range(SUB // 2)), tuple(range(SUB // 2, SUB))
    every = low + high
    ways = ((0, right, right2, low, high), (1, left, left2, high, low))

    def block(k, d, p):
        slot = (NZ - k) % NZ if d == 0 else k
        return protos.at[pl.ds(slot * B + p * PIECE, PIECE)]

    def ag_step(k):
        for i in range(SUB):
            for d, to1, to2, first, then in ways:
                p = (first + then)[i]
                if k > 0:
                    wait_recv(block(k, d, p), ag_rs.at[k - 1, d, p])
                if k == 2 and p in first:
                    copy(block(2, d, p), block(4, d, p), AG, far_ag_rs.at[d], to2).start()
                copy(block(k, d, p), block(k + 1, d, p), AG, ag_rs.at[k, d, p], to1).start()

    def ag_wait():
        for d in (0, 1):
            for p in every:
                wait_recv(block(3, d, p), ag_rs.at[2, d, p])

    def ag_wait_far():
        for d in (0, 1):
            wait_recv(protos.at[pl.ds(0, H)], far_ag_rs.at[d])

    hop, last = {}, {}
    crops = (teach, stud)

    def forward(w, j):
        ref = crops[w]
        copy(
            ref.at[pl.ds(2 * j * B, B)], ref.at[pl.ds((2 * j + 1) * B, B)], FORWARD + w, fw_rs.at[w], sibling
        ).start()

    def crop_start(w):
        ref = crops[w]
        for first in (0, 1):
            for d, to, j in ((0, up, 3), (1, down, 1)):
                h = first if d == 0 else 1 - first
                cp = copy(
                    ref.at[pl.ds(h * H, H)], ref.at[pl.ds(2 * j * B + h * H, H)],
                    CROP + w, hop_rs.at[w, d, h], to,
                )
                cp.start()
                hop[(w, d, h)] = cp
        forward(w, 0)

    def crop_relay(w):
        ref = crops[w]
        for d, to, j in ((0, up, 3), (1, down, 1)):
            hop[(w, d, d)].wait_recv()
            cp = copy(
                ref.at[pl.ds(2 * j * B + d * H, H)], ref.at[pl.ds(4 * B + d * H, H)],
                CROP + w, far_rs.at[w, d], to,
            )
            cp.start()
            last[(w, d)] = cp
        for d, j in ((0, 3), (1, 1)):
            hop[(w, d, 1 - d)].wait_recv()
            forward(w, j)

    def crop_last(w):
        for d in (0, 1):
            last[(w, d)].wait_recv()
        forward(w, 2)

    def crop_wait(w):
        wait_recv(crops[w].at[pl.ds(0, NY * B)], fw_rs.at[w])

    def teacher_slot(s):
        cols = slice(s * B, (s + 1) * B)
        dots = lax.dot_general(teach[...], protos[cols, :], NT, preferred_element_type=f32)
        values = jnp.exp2(dots * (LOG2E / teacher_temp))
        t_exp[:, cols] = values
        total = jnp.sum(values, axis=0, keepdims=True)
        for h in (0, 1):
            col_send[0, h, s:s + 1, :] = total[:, h * 128:(h + 1) * 128]

    def student_slot(s):
        cols = slice(s * B, (s + 1) * B)
        dots = lax.dot_general(stud[...], protos[cols, :], NT, preferred_element_type=f32)
        values = jnp.exp2(dots * (LOG2E / student_temp))
        s_exp[:, cols] = values
        both = values[:, :128] + values[:, 128:]
        part[...] = both if s == 0 else part[...] + both

    ag_step(0)
    crop_start(0)
    crop_start(1)
    ag_step(1)
    crop_relay(0)
    ag_step(2)
    crop_last(0)
    crop_wait(0)
    for s in (0, 1, 7, 2, 6):
        teacher_slot(s)
    crop_relay(1)
    ag_wait()
    teacher_slot(3)
    teacher_slot(5)
    ag_wait_far()
    teacher_slot(4)

    def tile(s, h):
        return slice(s * B + h * 128, s * B + (h + 1) * 128)

    def start_col(n, h):
        for o, peer in z_peers:
            copy(col_send.at[n, h], col_recv.at[n, h, NZ - o - 1], COL, col_rs.at[n, h], peer).start()

    def finish_col(n, h):
        total = col_send[n, h]
        wait_recv(col_recv.at[n, h], col_rs.at[n, h])
        for o in range(1, NZ):
            total = total + pltpu.roll(col_recv[n, h, o - 1], o, 0)
        return 1.0 / (PROTOS * total)

    def start_sibling(n, g):
        at = pl.ds(OFFSET[n], OFFSET[n + 1] - OFFSET[n])
        copy(row_sib.at[g, at], sib_recv.at[g, at], SIB, sib_rs.at[n, g], sibling).start()

    even = lax.broadcasted_iota(jnp.int32, (8, 128), 0) % 2 == 0

    def swap(v):
        return jnp.where(even, pltpu.roll(v, 7, 0), pltpu.roll(v, 1, 0))

    def start_row(n, g):
        start, height = OFFSET[n], OFFSET[n + 1] - OFFSET[n]
        at = pl.ds(start, height)
        wait_recv(sib_recv.at[g, at], sib_rs.at[n, g])
        for i in range(start, start + height, 8):
            row_send[g, i:i + 8, :] = row_sib[g, i:i + 8, :] + swap(sib_recv[g, i:i + 8, :])
        for (a, b), peer in yx_peers:
            t = ((NY - a) % NY) * NX + (NX - b) % NX - 1
            to = row_recv.at[g, pl.ds(N_YX * start + t * height, height)]
            copy(row_send.at[g, at], to, ROW, row_rs.at[n, g], peer).start()

    def finish_row(n, g):
        start, height = OFFSET[n], OFFSET[n + 1] - OFFSET[n]
        wait_recv(row_recv.at[g, pl.ds(N_YX * start, N_YX * height)], row_rs.at[n, g])
        out = []
        for i in range(0, height, 8):
            total = row_send[g, start + i:start + i + 8, :]
            for a in range(NY):
                some = None
                for b in range(NX):
                    if (a, b) == (0, 0):
                        continue
                    k = N_YX * start + (a * NX + b - 1) * height + i
                    v = row_recv[g, k:k + 8, :]
                    some = v if some is None else some + v
                total = total + (some if a == 0 else pltpu.roll(some, 2 * a, 0))
            out.append(total)
        return out

    lane = lax.broadcasted_iota(jnp.int32, (128, 128), 1)

    def half_rows(q, g):
        return pl.ds(pl.multiple_of(q * B + g * 128, 128), 128)

    def to_lanes(g, at):
        row_sib[g, at:at + 8, :] = jnp.transpose(mat[...])[0:8, :]

    def to_rows(v, g, out):
        wide = jnp.transpose(jnp.concatenate([v, jnp.zeros((120, 128), f32)], axis=0))
        for q in range(8):
            out[q * B + g * 128:q * B + (g + 1) * 128, :] = jnp.broadcast_to(wide[:, q:q + 1], (128, 128))

    def row_first(col, acc):
        for r in range(0, ROWS, 128):
            rows = slice(r, r + 128)
            total = t_exp[rows, tile(0, 0)] * col[0:1, :]
            for s in range(1, NZ):
                total = total + t_exp[rows, tile(s, 0)] * col[s:s + 1, :]
            acc[rows, :] = total

    def row_last(col, acc, g):
        wide = jnp.zeros((128, 128), f32)
        for q in range(8):
            rows = slice(q * B + g * 128, q * B + (g + 1) * 128)
            total = acc[rows, :]
            for s in range(NZ):
                total = total + t_exp[rows, tile(s, 1)] * col[s:s + 1, :]
            wide = jnp.where(lane == q, jnp.sum(total, axis=1, keepdims=True), wide)
        mat[...] = wide

    def partition_sum(g):
        mat[...] = jnp.zeros((128, 128), f32)

        def body(q, _):
            total = jnp.sum(part[half_rows(q, g), :], axis=1, keepdims=True)
            mat[...] = jnp.where(lane == q, total, mat[...])
            return 0

        lax.fori_loop(0, 8, body, 0)

    def col_part(g, acc, tiles):
        for q in range(8):
            rows = slice(q * B + g * 128, q * B + (g + 1) * 128)
            scale = row_b[rows, :]
            acc = tuple(
                v + jnp.sum((t_exp[rows, at] * scale).reshape(16, 8, 128), axis=0) for v, at in zip(acc, tiles)
            )
        return acc

    def row_to_col(n):
        zeros = jnp.zeros((8, 128), f32)
        both = [tile(s, h) for h in (0, 1) for s in range(NZ)]
        first = finish_row(n, 0)
        to_rows(1.0 / (CROPS * first[0]), 0, row_b)
        acc = col_part(0, (zeros,) * 16, both)
        second = finish_row(n, 1)
        to_rows(1.0 / (CROPS * second[0]), 1, row_b)
        for h in (0, 1):
            for s, v in enumerate(col_part(1, acc[h * 8:h * 8 + 8], both[h * 8:h * 8 + 8])):
                col_send[n + 1, h, s:s + 1, :] = jnp.sum(v, axis=0, keepdims=True)
            start_col(n + 1, h)
        return first[1:] + second[1:]

    def col_to_row(n, acc):
        first = finish_col(n, 0)
        row_first(first, acc)
        second = finish_col(n, 1)
        for g in (0, 1):
            row_last(second, acc, g)
            to_lanes(g, OFFSET[n])
            start_sibling(n, g)
        for g in (0, 1):
            start_row(n, g)
        return first, second

    start_col(0, 0)
    start_col(0, 1)
    crop_last(1)
    crop_wait(1)
    for s in range(4):
        student_slot(s)
    col_to_row(0, row_a)
    for s in range(4, 8):
        student_slot(s)
    row_to_col(0)
    for g in (0, 1):
        partition_sum(g)
        to_lanes(g, OFFSET[1] + 8)
    for q in range(8):
        stud_t[:, q * B:(q + 1) * B] = jnp.transpose(stud[q * B:(q + 1) * B, :].astype(f32)).astype(bf16)
    col_to_row(1, row_a)
    partition = row_to_col(1)
    for g in (0, 1):
        to_rows((loss_scale / student_temp) / partition[g], g, row_a)

    def scale_student(i, _):
        rows = pl.ds(pl.multiple_of(i * 64, 64), 64)
        scale = row_a[rows, :]
        for s in range(NZ):
            for h in (0, 1):
                s_exp[rows, tile(s, h)] = s_exp[rows, tile(s, h)] * scale
        return 0

    lax.fori_loop(0, ROWS // 64, scale_student, 0)
    col = col_to_row(2, part)

    def scale_teacher(i, _):
        rows = pl.ds(pl.multiple_of(i * 64, 64), 64)
        for s in range(NZ):
            for h in (0, 1):
                t_exp[rows, tile(s, h)] = t_exp[rows, tile(s, h)] * col[h][s:s + 1, :]
        return 0

    lax.fori_loop(0, ROWS // 64, scale_teacher, 0)
    for g in (0, 1):
        (row_total,) = finish_row(2, g)
        to_rows((loss_scale / student_temp) / row_total, g, row_b)

    def grad_part(start, height, slots):
        for r in range(start, start + height, 16):
            rows = slice(r, r + 16)
            scale = row_b[rows, :]
            for s in slots:
                for h in (0, 1):
                    at = tile(s, h)
                    grad[rows, at] = (s_exp[rows, at] - t_exp[rows, at] * scale).astype(bf16)

    def chunk_dot(s):
        chunk[s] = jnp.dot(stud_t[...], grad[:, s * B:(s + 1) * B], preferred_element_type=f32)

    def ring(m, d):
        s = 4 - m if d == 0 else 4 + m
        _, to1, to2, first, then = ways[d]
        for p in first if m == 0 else first + then:
            rows = slice(p * PIECE, (p + 1) * PIECE)
            at = pl.ds(p * PIECE, PIECE)
            value = chunk[s, rows, :]
            if m >= 2:
                wait_recv(ring_recv.at[2 * (m - 1) + d, at], rg_rs.at[m - 1, d, p])
                value = value + ring_recv[2 * (m - 1) + d, rows, :].astype(f32)
            if m == 2 and p in first:
                wait_recv(ring_recv.at[d, at], rg_rs.at[0, d, p])
                value = value + ring_recv[d, rows, :].astype(f32)
            ring_send[2 * m + d, rows, :] = value.astype(bf16)
            copy(
                ring_send.at[2 * m + d, at], ring_recv.at[2 * m + d, at], RING, rg_rs.at[m, d, p],
                to2 if m == 0 else to1,
            ).start()

    def u_dot(q):
        return jnp.dot(grad[q * B:(q + 1) * B, :], protos[...], preferred_element_type=f32)

    us = {}

    def u_grad(j, slots):
        grad_part((2 * j + 1) * B, B, slots)
        grad_part(2 * j * B, B, slots)

    def u_pair(j):
        u_send[j] = u_dot(2 * j + 1).astype(bf16)
        u_ref[j] = u_dot(2 * j)

    def u_start(j):
        cp = copy(u_send.at[j], u_sib.at[j], US, us_rs.at[j], sibling)
        cp.start()
        us[j] = cp

    Q = B // NX
    mine = pl.ds(pl.multiple_of(x * Q, Q), Q)

    def v_start(j):
        us[j].wait_recv()
        total = u_ref[j] + u_sib[j].astype(f32)
        if j == 0:
            u_ref[j] = total
        v_send[j] = total.astype(bf16)
        for b in (2, 1, 3, 0):
            if (j, b) == (0, 0):
                continue
            t = ((NY - j) % NY) * NX + (NX - b) % NX - 1
            at = pl.multiple_of(((x + b) % NX) * Q, Q)
            copy(v_send.at[j, pl.ds(at, Q)], v_recv.at[t], V, vq_rs.at[0], dev(0, j, 0, b)).start()

    rest = (0, 1, 2, 6, 7)
    grad_part(0, ROWS, (3,))
    chunk_dot(3)
    grad_part(0, ROWS, (5,))
    ring(1, 0)
    chunk_dot(5)
    grad_part(0, ROWS, (4,))
    ring(1, 1)
    chunk_dot(4)
    u_grad(2, rest)
    ring(0, 0)
    ring(0, 1)
    u_pair(2)
    u_grad(1, rest)
    u_start(2)
    u_pair(1)
    u_grad(3, rest)
    u_start(1)
    v_start(2)
    u_pair(3)
    u_grad(0, rest)
    u_start(3)
    v_start(1)
    u_pair(0)
    u_start(0)
    v_start(3)
    chunk_dot(2)
    chunk_dot(6)
    chunk_dot(1)
    v_start(0)
    ring(2, 0)
    ring(2, 1)
    chunk_dot(7)
    chunk_dot(0)
    ring(3, 0)
    ring(3, 1)

    wait_recv(v_recv, vq_rs.at[0])
    total = u_ref[0, mine, :]
    for i in range(N_YX):
        total = total + v_recv[i].astype(f32)
    unit, inverse = unit_rows(student_ref[mine, :])
    q_full[mine, :] = (inverse * (total - unit * jnp.sum(unit * total, axis=1, keepdims=True))).astype(bf16)
    for b in (2, 1, 3):
        copy(q_full.at[mine], q_full.at[mine], QS, vq_rs.at[1], dev(0, 0, 0, b)).start()

    total = chunk[0]
    for d in (0, 1):
        for p in every:
            wait_recv(ring_recv.at[6 + d, pl.ds(p * PIECE, PIECE)], rg_rs.at[3, d, p])
        total = total + ring_recv[6 + d].astype(f32)
    total = jnp.transpose(total)
    unit, inverse = unit_rows(proto_ref[...])
    gp_ref[...] = inverse * (total - unit * jnp.sum(unit * total, axis=1, keepdims=True))

    wait_recv(q_full.at[pl.ds(0, (NX - 1) * Q)], vq_rs.at[1])
    gs_ref[...] = q_full[...].astype(f32)

    wait_send(protos.at[pl.ds(0, 7 * B)], AG)
    for w in (0, 1):
        wait_send(crops[w].at[pl.ds(0, 3 * B)], CROP + w)
        wait_send(crops[w].at[pl.ds(0, 4 * B)], FORWARD + w)
    wait_send(col_recv, COL)
    wait_send(row_sib, SIB)
    wait_send(row_recv, ROW)
    wait_send(ring_recv.at[pl.ds(0, 7)], RING)
    wait_send(u_sib, US)
    wait_send(v_recv, V)
    wait_send(q_full.at[pl.ds(0, (NX - 1) * Q)], QS)


def shards(student_feat, teacher_feat, prototypes):
    vmem = pltpu.VMEM
    dma = pltpu.SemaphoreType.DMA
    sems = [
        dma((GROUPS,)), dma((3, 2, SUB)), dma((2,)), dma((2, 2, 2)), dma((2, 2)), dma((2,)), dma((SWEEPS, 2)), dma((SWEEPS, 2)),
        dma((SWEEPS, 2)), dma((4, 2, SUB)), dma((NY,)), dma((2,)),
    ]
    return pl.pallas_call(
        kernel,
        out_shape=[jax.ShapeDtypeStruct((B, B), f32), jax.ShapeDtypeStruct((B, B), f32)],
        in_specs=[pl.BlockSpec(memory_space=pltpu.VMEM)] * 3,
        out_specs=[pl.BlockSpec(memory_space=pltpu.VMEM)] * 2,
        scratch_shapes=[
            vmem((COLS, B), bf16),
            vmem((ROWS, B), bf16),
            vmem((ROWS, B), bf16),
            vmem((B, ROWS), bf16),
            vmem((ROWS, COLS), f32),
            vmem((ROWS, COLS), f32),
            vmem((ROWS, COLS), bf16),
            vmem((ROWS, 128), f32),
            vmem((ROWS, 128), f32),
            vmem((ROWS, 128), f32),
            vmem((128, 128), f32),
            vmem((SWEEPS, 2, 8, 128), f32),
            vmem((SWEEPS, 2, NZ - 1, 8, 128), f32),
            vmem((2, OFFSET[-1], 128), f32),
            vmem((2, OFFSET[-1], 128), f32),
            vmem((2, OFFSET[-1], 128), f32),
            vmem((2, N_YX * OFFSET[-1], 128), f32),
            vmem((NZ, B, B), f32),
            vmem((8, B, B), bf16),
            vmem((8, B, B), bf16),
            vmem((NY, B, B), f32),
            vmem((NY, B, B), bf16),
            vmem((NY, B, B), bf16),
            vmem((NY, B, B), bf16),
            vmem((N_YX, B // NX, B), bf16),
            vmem((B, B), bf16),
        ] + sems,
        compiler_params=pltpu.CompilerParams(
            collective_id=0, has_side_effects=True, vmem_limit_bytes=63 * 2**20
        ),
    )(student_feat, teacher_feat, prototypes)


def solution(mesh):
    in_specs = (P("dp", None), P("dp", None), P(("dp", "proto"), None))
    out_specs = (P("dp", None), P(("dp", "proto"), None))
    return jax.shard_map(shards, mesh=mesh, in_specs=in_specs, out_specs=out_specs, check_vma=False)
```
